32 devices in a mesh: blk: 8 (over y, x, core), grp: 4 (over z).
Axes of the slice: x: 2, y: 2, z: 4, core: 2. Of those that a mesh axis runs over, the one named last changes fastest.
Arguments:
- picture_embedding_array: bfloat16 [8192, 1152], P(('blk', 'grp')), may hold values from -0.1875 to 0.1875
- caption_embedding_array: bfloat16 [8192, 1152], P(('blk', 'grp')), may hold values from -0.1875 to 0.1875
- sharpness_multiplier: float32 [1], replicated, may hold values from 8 to 16
- score_offset: float32 [1], replicated, may hold values from -6 to -3
Outputs:
- row_loss: float32 [8192], P(('blk', 'grp'))
- grad_images: float32 [8192, 1152], P(('blk', 'grp'))
- grad_texts: float32 [8192, 1152], P(('blk', 'grp'))
The draws below stay inside these ranges and needn't reach their ends.
All inputs are finite; a program needn't handle non-finite values.
Results may differ from the reference program's by a relative error of at most 0.02.
Values may be sent and summed in bfloat16 or wider, within the bound.
A program may use at most 64 MiB of HBM per device.

```python
import jax
import jax.numpy as jnp
from jax import lax

D = 1152
ROWS = 256
KSTEPS = 8
PAIRS = 8192


def shard_levels(key, extent, shards, smallest, high):
    loudness = 1.0
    for axis_at, blocks in shards:
        steps = jax.random.uniform(jax.random.fold_in(jax.random.fold_in(key, 6), axis_at), (blocks,), jnp.float32, smallest / len(shards), high / len(shards))
        loudness = loudness * jnp.repeat(jnp.exp(steps), extent[axis_at] // blocks).reshape((-1,) + (1,) * (len(extent) - 1 - axis_at))
    return loudness


def noise(key, dims, deviation, reach, split=(), kind=jnp.bfloat16):
    gain = shard_levels(key, dims, split, -0.22, 0.18) if split else 1.0
    result = jax.random.normal(key, dims, jnp.float32) * deviation * gain
    return jnp.minimum(jnp.maximum(result, -reach), reach).astype(kind)


def setup_inputs(seed: int = 0) -> dict:
    splits = jax.random.split(jax.random.key(seed), 5)
    return {
        "picture_embedding_array": noise(splits[0], (PAIRS, D), D ** -0.5, 0.1875, ((0, 32),)),
        "caption_embedding_array": noise(splits[1], (PAIRS, D), D ** -0.5, 0.1875, ((0, 32),)),
        "sharpness_multiplier": jnp.clip(jax.random.uniform(splits[2], (1,), jnp.float32, 8.0, 16.0), 8.0, 16.0),
        "score_offset": jnp.clip(jax.random.uniform(splits[3], (1,), jnp.float32, -6.0, -3.0), -6.0, -3.0),
    }


def normalize(raw):
    computed_quantities = raw.astype(jnp.float32)
    inverse = lax.rsqrt(lax.optimization_barrier(jnp.sum(computed_quantities * computed_quantities, axis=-1, keepdims=True)) + 1e-06)
    return (computed_quantities * inverse, inverse)

def unrounded_value(unit32):
    rounded = lax.optimization_barrier(unit32.astype(jnp.bfloat16))
    return rounded.astype(jnp.float32)

def back_norm(unit32, inverse, grad_unit):
    along = lax.optimization_barrier(jnp.sum(unit32 * grad_unit, axis=-1, keepdims=True))
    return inverse * (grad_unit - unit32 * along)

def reference(picture_embedding_array, caption_embedding_array, sharpness_multiplier, score_offset):
    smoothing_coefficient = sharpness_multiplier[0]
    block_displacement = score_offset[0]
    img_unit32, img_inverse = normalize(picture_embedding_array)
    txt_unit32, txt_inverse = normalize(caption_embedding_array)
    blocks = picture_embedding_array.shape[0] // ROWS
    image_unit_vectors = unrounded_value(img_unit32).reshape(blocks, ROWS, D)
    text_unit_vectors = unrounded_value(txt_unit32).reshape(blocks, ROWS, D)
    diagonal_mask = jnp.eye(ROWS, dtype=jnp.float32) > 0.5
    row_total_sum = jnp.zeros((blocks, ROWS), jnp.float32)
    grad_img = jnp.zeros((blocks, ROWS, D), jnp.float32)
    grad_txt = jnp.zeros((blocks, ROWS, D), jnp.float32)
    for hop_index in range(KSTEPS):
        rotated_blocks = jnp.roll(text_unit_vectors, hop_index, axis=0)
        pair_logit_matrix = smoothing_coefficient * jnp.einsum('clu,cxu->clx', image_unit_vectors, rotated_blocks) + block_displacement
        if hop_index == 0:
            target_labels = jnp.where(diagonal_mask, 1.0, -1.0).astype(jnp.float32)
        else:
            target_labels = jnp.full((ROWS, ROWS), -1.0, jnp.float32)
        row_total_sum = row_total_sum + lax.optimization_barrier(jnp.sum(jax.nn.softplus(-target_labels * pair_logit_matrix), axis=-1))
        sigmoid_weights = unrounded_value(-target_labels * jax.nn.sigmoid(-target_labels * pair_logit_matrix) * smoothing_coefficient)
        grad_img = grad_img + jnp.einsum('mrs,msd->mrd', sigmoid_weights, rotated_blocks)
        grad_txt = grad_txt + jnp.roll(jnp.einsum('mrs,mrd->msd', sigmoid_weights, image_unit_vectors), -hop_index, axis=0)
    grad_images = back_norm(img_unit32, img_inverse, grad_img.reshape(-1, D))
    grad_texts = back_norm(txt_unit32, txt_inverse, grad_txt.reshape(-1, D))
    return (row_total_sum.reshape(-1), grad_images, grad_texts)
```

```python
import functools

import jax
import jax.numpy as jnp
from jax import lax
from jax.experimental import pallas as pl
from jax.experimental.pallas import tpu as pltpu
from jax.sharding import PartitionSpec as P

KSTEPS = 8


def passed_along(block, axis, distance):
    devices = range(lax.axis_size(axis))
    route = [((i - distance) % len(devices), i) for i in devices]
    return lax.ppermute(block, axis, route)


def normalize(raw):
    computed_quantities = raw.astype(jnp.float32)
    inverse = lax.rsqrt(
        jnp.sum(computed_quantities * computed_quantities, axis=-1, keepdims=True) + 1e-06
    )
    return (computed_quantities * inverse, inverse)


def back_norm(unit32, inverse, grad_unit):
    along = jnp.sum(unit32 * grad_unit, axis=-1, keepdims=True)
    return inverse * (grad_unit - unit32 * along)


def pairwise_loss_terms(
    image_block_rows, text_block_rows, target_labels, smoothing_coefficient, block_displacement
):
    pair_logit_matrix = (
        smoothing_coefficient
        * lax.dot_general(
            image_block_rows,
            text_block_rows,
            (((1,), (1,)), ((), ())),
            preferred_element_type=jnp.float32,
        )
        + block_displacement
    )
    row_portion = jnp.sum(jax.nn.softplus(-target_labels * pair_logit_matrix), axis=-1)
    sigmoid_weights = (
        -target_labels * jax.nn.sigmoid(-target_labels * pair_logit_matrix) * smoothing_coefficient
    ).astype(jnp.bfloat16)
    return (row_portion, sigmoid_weights)


def image_side(sigmoid_weights, text_block_rows):
    return jnp.dot(sigmoid_weights, text_block_rows, preferred_element_type=jnp.float32)


def text_side(sigmoid_weights, image_block_rows):
    return lax.dot_general(
        sigmoid_weights,
        image_block_rows,
        (((0,), (0,)), ((), ())),
        preferred_element_type=jnp.float32,
    )


def on_device(picture_embedding_array, caption_embedding_array, sharpness_multiplier, score_offset):
    smoothing_coefficient = sharpness_multiplier[0]
    block_displacement = score_offset[0]
    rows = picture_embedding_array.shape[0]
    img_unit32, img_inverse = normalize(picture_embedding_array)
    txt_unit32, txt_inverse = normalize(caption_embedding_array)
    image_unit_vectors = img_unit32.astype(jnp.bfloat16)
    text_unit_vectors = txt_unit32.astype(jnp.bfloat16)
    positions = lax.broadcasted_iota(jnp.int32, (rows, rows), 0)
    columns = lax.broadcasted_iota(jnp.int32, (rows, rows), 1)
    initial_label_values = jnp.where(positions == columns, 1.0, -1.0).astype(jnp.float32)
    negative_labels = jnp.full((rows, rows), -1.0, jnp.float32)
    row_total_sum, sigmoid_weights = pairwise_loss_terms(
        image_unit_vectors,
        text_unit_vectors,
        initial_label_values,
        smoothing_coefficient,
        block_displacement,
    )
    grad_img = image_side(sigmoid_weights, text_unit_vectors)
    own_text = text_side(sigmoid_weights, image_unit_vectors)
    incoming_caption_groups = text_unit_vectors
    carried = own_text
    for hop_index in range(1, KSTEPS):
        incoming_caption_groups, carried = (
            passed_along(incoming_caption_groups, ("blk", "grp"), 1),
            passed_along(carried.astype(jnp.bfloat16), ("blk", "grp"), 1).astype(carried.dtype),
        )
        row_portion, sigmoid_weights = pairwise_loss_terms(
            image_unit_vectors,
            incoming_caption_groups,
            negative_labels,
            smoothing_coefficient,
            block_displacement,
        )
        row_total_sum = row_total_sum + row_portion
        grad_img = grad_img + image_side(sigmoid_weights, incoming_caption_groups)
        carried = carried + text_side(sigmoid_weights, image_unit_vectors)
    grad_txt = passed_along(carried.astype(jnp.bfloat16), ("blk", "grp"), 1 - KSTEPS).astype(
        carried.dtype
    )
    grad_images = back_norm(img_unit32, img_inverse, grad_img)
    grad_texts = back_norm(txt_unit32, txt_inverse, grad_txt)
    return (row_total_sum, grad_images, grad_texts)


MESH = pl.DeviceIdType.MESH
A_NEAR, B_NEAR, X_NEAR, A_FAR, B_FAR, F_FAR = range(6)
KINDS = 6
A_UP, A_DOWN, B_UP, B_DOWN, A_CORE, A_COLUMN, B_COLUMN, F_CORE = range(8)
SENDS = 8
LANES = 128


def column_kernel(
    columns,
    deep,
    scale_ref,
    offset_ref,
    img_ref,
    txt_ref,
    loss_ref,
    grad_img_ref,
    grad_txt_ref,
    held,
    total,
    losses,
    send_sem,
    recv_sem,
):
    blk = lax.axis_index("blk")
    z = lax.axis_index("grp")
    core = lax.rem(blk, 2)
    column = blk // 2
    onward = 1 - 2 * core
    after = lax.rem(column + onward + columns, columns)
    before = lax.rem(column - onward + columns, columns)
    sibling = (2 * column + 1 - core, z)
    above, below = (blk, z + 1), (blk, z - 1)
    after_same = (2 * after + core, z)
    before_same = (2 * before + core, z)
    before_other = (2 * before + 1 - core, z)
    rows, width = img_ref.shape
    scale, offset = scale_ref[0], offset_ref[0]

    def beyond(zp):
        return (zp - z) * onward > 0

    def short(zp):
        return (zp - z) * onward < 0

    def slot(kind, zp):
        return kind * deep + zp

    def transfer(send, source, target, zp, device):
        return pltpu.make_async_remote_copy(
            src_ref=held.at[slot(source, zp)],
            dst_ref=held.at[slot(target, zp)],
            send_sem=send_sem.at[send * deep + zp],
            recv_sem=recv_sem.at[slot(target, zp)],
            device_id=device,
            device_id_type=MESH,
        )

    def arrived(kind, zp):
        transfer(A_UP, kind, kind, zp, sibling).wait_recv()

    def sent(send, zp):
        transfer(send, A_NEAR, A_NEAR, zp, sibling).wait_send()

    def unit(ref):
        raw = ref[...].astype(jnp.float32)
        inverse = lax.rsqrt(jnp.sum(raw * raw, axis=-1, keepdims=True) + 1e-06)
        return raw * inverse, inverse

    @pl.when(core == 0)
    def _():
        held[slot(A_NEAR, z)] = unit(txt_ref)[0].astype(jnp.bfloat16)
        held[slot(B_NEAR, z)] = unit(img_ref)[0].astype(jnp.bfloat16)

    @pl.when(core == 1)
    def _():
        held[slot(A_NEAR, z)] = unit(img_ref)[0].astype(jnp.bfloat16)
        held[slot(B_NEAR, z)] = unit(txt_ref)[0].astype(jnp.bfloat16)

    barrier = pltpu.get_barrier_semaphore()
    for device in (sibling, after_same, before_same, before_other):
        pl.semaphore_signal(barrier, inc=1, device_id=device, device_id_type=MESH)

    @pl.when(z < deep - 1)
    def _():
        pl.semaphore_signal(barrier, inc=1, device_id=above, device_id_type=MESH)

    @pl.when(z > 0)
    def _():
        pl.semaphore_signal(barrier, inc=1, device_id=below, device_id_type=MESH)

    total[...] = jnp.zeros_like(total)
    losses[...] = jnp.zeros_like(losses)
    edges = jnp.where(z > 0, 1, 0) + jnp.where(z < deep - 1, 1, 0)
    pl.semaphore_wait(barrier, 4 + edges)

    def pass_on(zp, distance):
        def along(up, down, kind):
            @pl.when((zp <= z) & (z < deep - 1))
            def _():
                transfer(up, kind, kind, zp, above).start()

            @pl.when((zp >= z) & (z > 0))
            def _():
                transfer(down, kind, kind, zp, below).start()

        @pl.when(distance > 0)
        def _():
            arrived(A_NEAR, zp)

        along(A_UP, A_DOWN, A_NEAR)

        @pl.when(beyond(zp))
        def _():
            transfer(A_COLUMN, A_NEAR, A_FAR, zp, after_same).start()

        transfer(A_CORE, A_NEAR, X_NEAR, zp, sibling).start()

        @pl.when(distance > 0)
        def _():
            arrived(B_NEAR, zp)

        along(B_UP, B_DOWN, B_NEAR)
        transfer(B_COLUMN, B_NEAR, B_FAR, zp, before_other).start()

    diagonal = lax.broadcasted_iota(jnp.int32, (rows, rows), 0) == lax.broadcasted_iota(
        jnp.int32, (rows, rows), 1
    )

    def meet(role, own, other, same):
        logits = (
            scale
            * lax.dot_general(
                held[own],
                held[other],
                (((1,), (1,)), ((), ())),
                preferred_element_type=jnp.float32,
            )
            + offset
        )
        sign = jnp.where(diagonal & same, -1.0, 1.0)
        turned = sign * logits
        small = jnp.exp(-jnp.abs(turned))
        loss = jnp.maximum(turned, 0.0) + jnp.log1p(small)
        sigmoid = jnp.where(turned >= 0.0, 1.0, small) / (1.0 + small)
        weights = (sign * sigmoid * scale).astype(jnp.bfloat16)
        part = loss[:, :LANES]
        for at in range(LANES, rows, LANES):
            part = part + loss[:, at : at + LANES]
        losses[role] += part
        step = 384 if width % 384 == 0 else width
        for at in range(0, width, step):
            total[role, :, at : at + step] += jnp.dot(
                weights, held[other, :, at : at + step], preferred_element_type=jnp.float32
            )

    def work(zp):
        arrived(B_FAR, zp)

        @pl.when(beyond(zp))
        def _():
            transfer(F_CORE, B_FAR, F_FAR, zp, sibling).start()
            arrived(A_FAR, zp)

        arrived(X_NEAR, zp)

        @pl.when(short(zp))
        def _():
            arrived(F_FAR, zp)

        def tile(which, carry):
            role = which // 2
            kind_p = jnp.where(beyond(zp), A_FAR, A_NEAR)
            kind_q = jnp.where(short(zp), F_FAR, B_NEAR)
            kind = jnp.where(
                which == 0,
                kind_p,
                jnp.where(which == 1, B_FAR, jnp.where(which == 2, kind_q, X_NEAR)),
            )
            own = jnp.where(role == 0, slot(B_NEAR, z), slot(A_NEAR, z))
            meet(role, own, slot(kind, zp), (lax.rem(which, 2) == 0) & (zp == z))
            return carry

        lax.fori_loop(0, 4, tile, 0)

    def both_ways(distance, action):
        @pl.when(z - distance >= 0)
        def _():
            action(z - distance)

        @pl.when((distance > 0) & (z + distance < deep))
        def _():
            action(z + distance)

    def turn(distance, carry):
        @pl.when(distance < deep)
        def _():
            both_ways(distance, lambda zp: pass_on(zp, distance))

        @pl.when(distance > 0)
        def _():
            @pl.when(z - distance + 1 >= 0)
            def _():
                work(z - distance + 1)

            @pl.when((distance > 1) & (z + distance - 1 < deep))
            def _():
                work(z + distance - 1)

        return carry

    lax.fori_loop(0, deep + 1, turn, 0)

    def finish(ref, role):
        unit32, inverse = unit(ref)
        grad = total[role]
        along = jnp.sum(unit32 * grad, axis=-1, keepdims=True)
        return inverse * (grad - unit32 * along)

    grad_img_ref[...] = finish(img_ref, core)
    grad_txt_ref[...] = finish(txt_ref, 1 - core)
    loss_ref[...] = jnp.sum(losses[core], axis=-1, keepdims=True)

    def settle(zp, carry):
        @pl.when((zp <= z) & (z < deep - 1))
        def _():
            sent(A_UP, zp)
            sent(B_UP, zp)

        @pl.when((zp >= z) & (z > 0))
        def _():
            sent(A_DOWN, zp)
            sent(B_DOWN, zp)

        @pl.when(beyond(zp))
        def _():
            sent(A_COLUMN, zp)
            sent(F_CORE, zp)

        sent(A_CORE, zp)
        sent(B_COLUMN, zp)
        return carry

    lax.fori_loop(0, deep, settle, 0)


def on_column(columns, deep, images, texts, scale, offset):
    rows, width = images.shape
    tiles = 4 * deep
    loss, grad_images, grad_texts = pl.pallas_call(
        functools.partial(column_kernel, columns, deep),
        out_shape=(
            jax.ShapeDtypeStruct((rows, 1), jnp.float32),
            jax.ShapeDtypeStruct((rows, width), jnp.float32),
            jax.ShapeDtypeStruct((rows, width), jnp.float32),
        ),
        in_specs=[pl.BlockSpec(memory_space=pltpu.SMEM)] * 2
        + [pl.BlockSpec(memory_space=pltpu.VMEM)] * 2,
        out_specs=[pl.BlockSpec(memory_space=pltpu.VMEM)] * 3,
        scratch_shapes=[
            pltpu.VMEM((KINDS * deep, rows, width), jnp.bfloat16),
            pltpu.VMEM((2, rows, width), jnp.float32),
            pltpu.VMEM((2, rows, LANES), jnp.float32),
            pltpu.SemaphoreType.DMA((SENDS * deep,)),
            pltpu.SemaphoreType.DMA((KINDS * deep,)),
        ],
        compiler_params=pltpu.CompilerParams(
            collective_id=0, has_side_effects=True, vmem_limit_bytes=48 * 1024 * 1024
        ),
        cost_estimate=pl.CostEstimate(
            flops=tiles * 4 * rows * rows * width,
            bytes_accessed=12 * rows * width,
            transcendentals=tiles * 3 * rows * rows,
        ),
        name="column",
    )(scale, offset, images, texts)
    return loss.reshape(rows), grad_images, grad_texts


def solution(mesh):
    blocks, deep = mesh.shape["blk"], mesh.shape["grp"]
    body = on_device
    if KSTEPS == 2 * deep and blocks % 2 == 0 and blocks >= 6:
        body = functools.partial(on_column, blocks // 2, deep)
    return jax.shard_map(
        body,
        mesh=mesh,
        in_specs=(P(("blk", "grp"), None), P(("blk", "grp"), None), P(), P()),
        out_specs=(P(("blk", "grp")), P(("blk", "grp"), None), P(("blk", "grp"), None)),
        check_vma=False,
    )
```

```python
import functools

import jax
import jax.numpy as jnp
from jax import lax
from jax.experimental import pallas as pl
from jax.experimental.pallas import tpu as pltpu
from jax.sharding import PartitionSpec as P

KSTEPS = 8


def passed_along(block, axis, distance):
    devices = range(lax.axis_size(axis))
    route = [((i - distance) % len(devices), i) for i in devices]
    return lax.ppermute(block, axis, route)


def normalize(raw):
    computed_quantities = raw.astype(jnp.float32)
    inverse = lax.rsqrt(
        jnp.sum(computed_quantities * computed_quantities, axis=-1, keepdims=True) + 1e-06
    )
    return (computed_quantities * inverse, inverse)


def back_norm(unit32, inverse, grad_unit):
    along = jnp.sum(unit32 * grad_unit, axis=-1, keepdims=True)
    return inverse * (grad_unit - unit32 * along)


def pairwise_loss_terms(
    image_block_rows, text_block_rows, target_labels, smoothing_coefficient, block_displacement
):
    pair_logit_matrix = (
        smoothing_coefficient
        * lax.dot_general(
            image_block_rows,
            text_block_rows,
            (((1,), (1,)), ((), ())),
            preferred_element_type=jnp.float32,
        )
        + block_displacement
    )
    row_portion = jnp.sum(jax.nn.softplus(-target_labels * pair_logit_matrix), axis=-1)
    sigmoid_weights = (
        -target_labels * jax.nn.sigmoid(-target_labels * pair_logit_matrix) * smoothing_coefficient
    ).astype(jnp.bfloat16)
    return (row_portion, sigmoid_weights)


def image_side(sigmoid_weights, text_block_rows):
    return jnp.dot(sigmoid_weights, text_block_rows, preferred_element_type=jnp.float32)


def text_side(sigmoid_weights, image_block_rows):
    return lax.dot_general(
        sigmoid_weights,
        image_block_rows,
        (((0,), (0,)), ((), ())),
        preferred_element_type=jnp.float32,
    )


def on_device(picture_embedding_array, caption_embedding_array, sharpness_multiplier, score_offset):
    smoothing_coefficient = sharpness_multiplier[0]
    block_displacement = score_offset[0]
    rows = picture_embedding_array.shape[0]
    img_unit32, img_inverse = normalize(picture_embedding_array)
    txt_unit32, txt_inverse = normalize(caption_embedding_array)
    image_unit_vectors = img_unit32.astype(jnp.bfloat16)
    text_unit_vectors = txt_unit32.astype(jnp.bfloat16)
    positions = lax.broadcasted_iota(jnp.int32, (rows, rows), 0)
    columns = lax.broadcasted_iota(jnp.int32, (rows, rows), 1)
    initial_label_values = jnp.where(positions == columns, 1.0, -1.0).astype(jnp.float32)
    negative_labels = jnp.full((rows, rows), -1.0, jnp.float32)
    row_total_sum, sigmoid_weights = pairwise_loss_terms(
        image_unit_vectors,
        text_unit_vectors,
        initial_label_values,
        smoothing_coefficient,
        block_displacement,
    )
    grad_img = image_side(sigmoid_weights, text_unit_vectors)
    own_text = text_side(sigmoid_weights, image_unit_vectors)
    incoming_caption_groups = text_unit_vectors
    carried = own_text
    for hop_index in range(1, KSTEPS):
        incoming_caption_groups, carried = (
            passed_along(incoming_caption_groups, ("blk", "grp"), 1),
            passed_along(carried.astype(jnp.bfloat16), ("blk", "grp"), 1).astype(carried.dtype),
        )
        row_portion, sigmoid_weights = pairwise_loss_terms(
            image_unit_vectors,
            incoming_caption_groups,
            negative_labels,
            smoothing_coefficient,
            block_displacement,
        )
        row_total_sum = row_total_sum + row_portion
        grad_img = grad_img + image_side(sigmoid_weights, incoming_caption_groups)
        carried = carried + text_side(sigmoid_weights, image_unit_vectors)
    grad_txt = passed_along(carried.astype(jnp.bfloat16), ("blk", "grp"), 1 - KSTEPS).astype(
        carried.dtype
    )
    grad_images = back_norm(img_unit32, img_inverse, grad_img)
    grad_texts = back_norm(txt_unit32, txt_inverse, grad_txt)
    return (row_total_sum, grad_images, grad_texts)


MESH = pl.DeviceIdType.MESH
A_NEAR, B_NEAR, X_NEAR, A_FAR, B_FAR, F_FAR = range(6)
KINDS = 6
A_UP, A_DOWN, B_UP, B_DOWN, A_CORE, A_COLUMN, B_COLUMN, F_CORE = range(8)
SENDS = 8
LANES = 128
PARTS = 2


def column_kernel(
    columns,
    deep,
    scale_ref,
    offset_ref,
    img_ref,
    txt_ref,
    loss_ref,
    grad_img_ref,
    grad_txt_ref,
    held,
    total,
    losses,
    send_sem,
    recv_sem,
):
    blk = lax.axis_index("blk")
    z = lax.axis_index("grp")
    core = lax.rem(blk, 2)
    column = blk // 2
    onward = 1 - 2 * core
    after = lax.rem(column + onward + columns, columns)
    before = lax.rem(column - onward + columns, columns)
    sibling = (2 * column + 1 - core, z)
    above, below = (blk, z + 1), (blk, z - 1)
    after_same = (2 * after + core, z)
    before_same = (2 * before + core, z)
    before_other = (2 * before + 1 - core, z)
    rows, width = img_ref.shape
    scale, offset = scale_ref[0], offset_ref[0]

    def beyond(zp):
        return (zp - z) * onward > 0

    def short(zp):
        return (zp - z) * onward < 0

    def slot(kind, zp):
        return kind * deep + zp

    size = rows // PARTS

    def transfer(send, source, target, zp, device, part):
        here = pl.ds(part * size, size)
        return pltpu.make_async_remote_copy(
            src_ref=held.at[slot(source, zp), here],
            dst_ref=held.at[slot(target, zp), here],
            send_sem=send_sem.at[send * deep + zp, part],
            recv_sem=recv_sem.at[slot(target, zp), part],
            device_id=device,
            device_id_type=MESH,
        )

    def arrived(kind, zp, part):
        transfer(A_UP, kind, kind, zp, sibling, part).wait_recv()

    def sent(send, zp):
        for part in range(PARTS):
            transfer(send, A_NEAR, A_NEAR, zp, sibling, part).wait_send()

    def unit(ref):
        raw = ref[...].astype(jnp.float32)
        inverse = lax.rsqrt(jnp.sum(raw * raw, axis=-1, keepdims=True) + 1e-06)
        return raw * inverse, inverse

    @pl.when(core == 0)
    def _():
        held[slot(A_NEAR, z)] = unit(txt_ref)[0].astype(jnp.bfloat16)
        held[slot(B_NEAR, z)] = unit(img_ref)[0].astype(jnp.bfloat16)

    @pl.when(core == 1)
    def _():
        held[slot(A_NEAR, z)] = unit(img_ref)[0].astype(jnp.bfloat16)
        held[slot(B_NEAR, z)] = unit(txt_ref)[0].astype(jnp.bfloat16)

    barrier = pltpu.get_barrier_semaphore()
    for device in (sibling, after_same, before_same, before_other):
        pl.semaphore_signal(barrier, inc=1, device_id=device, device_id_type=MESH)

    @pl.when(z < deep - 1)
    def _():
        pl.semaphore_signal(barrier, inc=1, device_id=above, device_id_type=MESH)

    @pl.when(z > 0)
    def _():
        pl.semaphore_signal(barrier, inc=1, device_id=below, device_id_type=MESH)

    total[...] = jnp.zeros_like(total)
    losses[...] = jnp.zeros_like(losses)
    edges = jnp.where(z > 0, 1, 0) + jnp.where(z < deep - 1, 1, 0)
    pl.semaphore_wait(barrier, 4 + edges)

    def along(up, down, kind, zp, part):
        @pl.when((zp <= z) & (z < deep - 1))
        def _():
            transfer(up, kind, kind, zp, above, part).start()

        @pl.when((zp >= z) & (z > 0))
        def _():
            transfer(down, kind, kind, zp, below, part).start()

    def pass_b(zp, distance, part):
        @pl.when(distance > 0)
        def _():
            arrived(B_NEAR, zp, part)

        along(B_UP, B_DOWN, B_NEAR, zp, part)
        transfer(B_COLUMN, B_NEAR, B_FAR, zp, before_other, part).start()

    def pass_a(zp, distance, part):
        @pl.when(distance > 0)
        def _():
            arrived(A_NEAR, zp, part)

        along(A_UP, A_DOWN, A_NEAR, zp, part)

        @pl.when(beyond(zp))
        def _():
            transfer(A_COLUMN, A_NEAR, A_FAR, zp, after_same, part).start()

        transfer(A_CORE, A_NEAR, X_NEAR, zp, sibling, part).start()

    diagonal = lax.broadcasted_iota(jnp.int32, (rows, rows), 0) == lax.broadcasted_iota(
        jnp.int32, (rows, rows), 1
    )

    def meet(role, own, other, same):
        logits = (
            scale
            * lax.dot_general(
                held[own],
                held[other],
                (((1,), (1,)), ((), ())),
                preferred_element_type=jnp.float32,
            )
            + offset
        )
        sign = jnp.where(diagonal & same, -1.0, 1.0)
        turned = sign * logits
        small = jnp.exp(-jnp.abs(turned))
        loss = jnp.maximum(turned, 0.0) + jnp.log1p(small)
        sigmoid = jnp.where(turned >= 0.0, 1.0, small) / (1.0 + small)
        weights = (sign * sigmoid * scale).astype(jnp.bfloat16)
        part = loss[:, :LANES]
        for at in range(LANES, rows, LANES):
            part = part + loss[:, at : at + LANES]
        losses[role] += part
        step = 384 if width % 384 == 0 else width
        for at in range(0, width, step):
            total[role, :, at : at + step] += jnp.dot(
                weights, held[other, :, at : at + step], preferred_element_type=jnp.float32
            )

    own_a, own_b = slot(A_NEAR, z), slot(B_NEAR, z)

    def near(zp):
        first = jnp.where(short(zp), 0, jnp.where(beyond(zp), 1, 0))

        def tile(which, carry):
            @pl.when(which == 2)
            def _():
                for part in range(PARTS):
                    arrived(X_NEAR, zp, part)

            role = jnp.where(which == 0, 0, 1)
            kind = jnp.where(which == 0, A_NEAR, jnp.where(which == 1, B_NEAR, X_NEAR))
            own = jnp.where(which == 0, own_b, own_a)

            @pl.when((which == 2) | (which == first) | (zp == z))
            def _():
                meet(role, own, slot(kind, zp), (which < 2) & (zp == z))

            return carry

        lax.fori_loop(0, 3, tile, 0)

    def far(zp):
        for part in range(PARTS):
            arrived(B_FAR, zp, part)

            @pl.when(beyond(zp))
            def _():
                transfer(F_CORE, B_FAR, F_FAR, zp, sibling, part).start()

        def tile(which, carry):
            for part in range(PARTS):

                @pl.when((which == 1) & beyond(zp))
                def _():
                    arrived(A_FAR, zp, part)

                @pl.when((which == 1) & short(zp))
                def _():
                    arrived(F_FAR, zp, part)

            in_q = (which == 1) & short(zp)
            kind = jnp.where(which == 0, B_FAR, jnp.where(short(zp), F_FAR, A_FAR))

            @pl.when((which == 0) | (zp != z))
            def _():
                meet(
                    jnp.where(in_q, 1, 0),
                    jnp.where(in_q, own_a, own_b),
                    slot(kind, zp),
                    False,
                )

            return carry

        lax.fori_loop(0, 2, tile, 0)

    def both_ways(distance, action):
        @pl.when((distance >= 0) & (distance < deep) & (z - distance >= 0))
        def _():
            action(z - distance)

        @pl.when((distance > 0) & (z + distance < deep))
        def _():
            action(z + distance)

    def turn(distance, carry):
        for step in (pass_b, pass_a):
            for part in range(PARTS):
                both_ways(distance, functools.partial(step, distance=distance, part=part))
        both_ways(distance, near)
        both_ways(distance - 1, far)
        return carry

    lax.fori_loop(0, deep + 1, turn, 0)

    def finish(ref, role):
        unit32, inverse = unit(ref)
        grad = total[role]
        along = jnp.sum(unit32 * grad, axis=-1, keepdims=True)
        return inverse * (grad - unit32 * along)

    grad_img_ref[...] = finish(img_ref, core)
    grad_txt_ref[...] = finish(txt_ref, 1 - core)
    loss_ref[...] = jnp.sum(losses[core], axis=-1, keepdims=True)

    def settle(zp, carry):
        @pl.when((zp <= z) & (z < deep - 1))
        def _():
            sent(A_UP, zp)
            sent(B_UP, zp)

        @pl.when((zp >= z) & (z > 0))
        def _():
            sent(A_DOWN, zp)
            sent(B_DOWN, zp)

        @pl.when(beyond(zp))
        def _():
            sent(A_COLUMN, zp)
            sent(F_CORE, zp)

        sent(A_CORE, zp)
        sent(B_COLUMN, zp)
        return carry

    lax.fori_loop(0, deep, settle, 0)


def on_column(columns, deep, images, texts, scale, offset):
    rows, width = images.shape
    tiles = 4 * deep
    loss, grad_images, grad_texts = pl.pallas_call(
        functools.partial(column_kernel, columns, deep),
        out_shape=(
            jax.ShapeDtypeStruct((rows, 1), jnp.float32),
            jax.ShapeDtypeStruct((rows, width), jnp.float32),
            jax.ShapeDtypeStruct((rows, width), jnp.float32),
        ),
        in_specs=[pl.BlockSpec(memory_space=pltpu.SMEM)] * 2
        + [pl.BlockSpec(memory_space=pltpu.VMEM)] * 2,
        out_specs=[pl.BlockSpec(memory_space=pltpu.VMEM)] * 3,
        scratch_shapes=[
            pltpu.VMEM((KINDS * deep, rows, width), jnp.bfloat16),
            pltpu.VMEM((2, rows, width), jnp.float32),
            pltpu.VMEM((2, rows, LANES), jnp.float32),
            pltpu.SemaphoreType.DMA((SENDS * deep, PARTS)),
            pltpu.SemaphoreType.DMA((KINDS * deep, PARTS)),
        ],
        compiler_params=pltpu.CompilerParams(
            collective_id=0, has_side_effects=True, vmem_limit_bytes=48 * 1024 * 1024
        ),
        cost_estimate=pl.CostEstimate(
            flops=tiles * 4 * rows * rows * width,
            bytes_accessed=12 * rows * width,
            transcendentals=tiles * 3 * rows * rows,
        ),
        name="column",
    )(scale, offset, images, texts)
    return loss.reshape(rows), grad_images, grad_texts


def solution(mesh):
    blocks, deep = mesh.shape["blk"], mesh.shape["grp"]
    body = on_device
    if KSTEPS == 2 * deep and blocks % 2 == 0 and blocks >= 6:
        body = functools.partial(on_column, blocks // 2, deep)
    return jax.shard_map(
        body,
        mesh=mesh,
        in_specs=(P(("blk", "grp"), None), P(("blk", "grp"), None), P(), P()),
        out_specs=(P(("blk", "grp")), P(("blk", "grp"), None), P(("blk", "grp"), None)),
        check_vma=False,
    )
```

```python
import functools

import jax
import jax.numpy as jnp
from jax import lax
from jax.experimental import pallas as pl
from jax.experimental.pallas import tpu as pltpu
from jax.sharding import PartitionSpec as P

KSTEPS = 8


def passed_along(block, axis, distance):
    devices = range(lax.axis_size(axis))
    route = [((i - distance) % len(devices), i) for i in devices]
    return lax.ppermute(block, axis, route)


def normalize(raw):
    computed_quantities = raw.astype(jnp.float32)
    inverse = lax.rsqrt(
        jnp.sum(computed_quantities * computed_quantities, axis=-1, keepdims=True) + 1e-06
    )
    return (computed_quantities * inverse, inverse)


def back_norm(unit32, inverse, grad_unit):
    along = jnp.sum(unit32 * grad_unit, axis=-1, keepdims=True)
    return inverse * (grad_unit - unit32 * along)


def pairwise_loss_terms(
    image_block_rows, text_block_rows, target_labels, smoothing_coefficient, block_displacement
):
    pair_logit_matrix = (
        smoothing_coefficient
        * lax.dot_general(
            image_block_rows,
            text_block_rows,
            (((1,), (1,)), ((), ())),
            preferred_element_type=jnp.float32,
        )
        + block_displacement
    )
    row_portion = jnp.sum(jax.nn.softplus(-target_labels * pair_logit_matrix), axis=-1)
    sigmoid_weights = (
        -target_labels * jax.nn.sigmoid(-target_labels * pair_logit_matrix) * smoothing_coefficient
    ).astype(jnp.bfloat16)
    return (row_portion, sigmoid_weights)


def image_side(sigmoid_weights, text_block_rows):
    return jnp.dot(sigmoid_weights, text_block_rows, preferred_element_type=jnp.float32)


def text_side(sigmoid_weights, image_block_rows):
    return lax.dot_general(
        sigmoid_weights,
        image_block_rows,
        (((0,), (0,)), ((), ())),
        preferred_element_type=jnp.float32,
    )


def on_device(picture_embedding_array, caption_embedding_array, sharpness_multiplier, score_offset):
    smoothing_coefficient = sharpness_multiplier[0]
    block_displacement = score_offset[0]
    rows = picture_embedding_array.shape[0]
    img_unit32, img_inverse = normalize(picture_embedding_array)
    txt_unit32, txt_inverse = normalize(caption_embedding_array)
    image_unit_vectors = img_unit32.astype(jnp.bfloat16)
    text_unit_vectors = txt_unit32.astype(jnp.bfloat16)
    positions = lax.broadcasted_iota(jnp.int32, (rows, rows), 0)
    columns = lax.broadcasted_iota(jnp.int32, (rows, rows), 1)
    initial_label_values = jnp.where(positions == columns, 1.0, -1.0).astype(jnp.float32)
    negative_labels = jnp.full((rows, rows), -1.0, jnp.float32)
    row_total_sum, sigmoid_weights = pairwise_loss_terms(
        image_unit_vectors,
        text_unit_vectors,
        initial_label_values,
        smoothing_coefficient,
        block_displacement,
    )
    grad_img = image_side(sigmoid_weights, text_unit_vectors)
    own_text = text_side(sigmoid_weights, image_unit_vectors)
    incoming_caption_groups = text_unit_vectors
    carried = own_text
    for hop_index in range(1, KSTEPS):
        incoming_caption_groups, carried = (
            passed_along(incoming_caption_groups, ("blk", "grp"), 1),
            passed_along(carried.astype(jnp.bfloat16), ("blk", "grp"), 1).astype(carried.dtype),
        )
        row_portion, sigmoid_weights = pairwise_loss_terms(
            image_unit_vectors,
            incoming_caption_groups,
            negative_labels,
            smoothing_coefficient,
            block_displacement,
        )
        row_total_sum = row_total_sum + row_portion
        grad_img = grad_img + image_side(sigmoid_weights, incoming_caption_groups)
        carried = carried + text_side(sigmoid_weights, image_unit_vectors)
    grad_txt = passed_along(carried.astype(jnp.bfloat16), ("blk", "grp"), 1 - KSTEPS).astype(
        carried.dtype
    )
    grad_images = back_norm(img_unit32, img_inverse, grad_img)
    grad_texts = back_norm(txt_unit32, txt_inverse, grad_txt)
    return (row_total_sum, grad_images, grad_texts)


MESH = pl.DeviceIdType.MESH
A_NEAR, B_NEAR, X_NEAR, A_FAR, B_FAR, F_FAR = range(6)
KINDS = 6
A_UP, A_DOWN, B_UP, B_DOWN, A_CORE, A_COLUMN, B_COLUMN, F_CORE, A_RELAY, B_RELAY = range(10)
SENDS = 10
LANES = 128
PARTS = 2


def column_kernel(
    columns,
    deep,
    scale_ref,
    offset_ref,
    img_ref,
    txt_ref,
    loss_ref,
    grad_img_ref,
    grad_txt_ref,
    held,
    total,
    losses,
    sums,
    loss_in,
    send_sem,
    recv_sem,
    sum_sem,
):
    blk = lax.axis_index("blk")
    z = lax.axis_index("grp")
    core = lax.rem(blk, 2)
    column = blk // 2
    onward = 1 - 2 * core
    after = lax.rem(column + onward + columns, columns)
    before = lax.rem(column - onward + columns, columns)
    sibling = (2 * column + 1 - core, z)
    above, below = (blk, z + 1), (blk, z - 1)
    after_same = (2 * after + core, z)
    before_same = (2 * before + core, z)
    before_other = (2 * before + 1 - core, z)
    rows, width = img_ref.shape
    scale, offset = scale_ref[0], offset_ref[0]

    def beyond(zp):
        return (zp - z) * onward > 0

    def short(zp):
        return (zp - z) * onward < 0

    def slot(kind, zp):
        return kind * deep + zp

    at_end = (z == 0) | (z == deep - 1)
    a_end = jnp.where(onward > 0, z == deep - 1, z == 0)
    b_end = jnp.where(onward > 0, z == 0, z == deep - 1)
    q_helper = jnp.where(onward > 0, z == deep - 2, z == 1)
    p_helper = jnp.where(onward > 0, z == 1, z == deep - 2)
    helper = (z == 1) | (z == deep - 2)
    end = jnp.where(z == 1, 0, deep - 1)
    last = deep - 1 - end
    inner = (blk, jnp.where(z == 0, 1, deep - 2))
    outer = (blk, end)

    def has_a(zp):
        return (zp == z) | jnp.logical_not(b_end)

    def has_b(zp):
        return (zp == z) | jnp.logical_not(a_end)

    def a_goes_up(zp):
        return has_a(zp) & (zp <= z) & ((z < deep - 2) | ((z == deep - 2) & (onward > 0)))

    def a_goes_down(zp):
        return has_a(zp) & (zp >= z) & ((z > 1) | ((z == 1) & (onward < 0)))

    def b_goes_up(zp):
        return has_b(zp) & (zp <= z) & ((z < deep - 2) | ((z == deep - 2) & (onward < 0)))

    def b_goes_down(zp):
        return has_b(zp) & (zp >= z) & ((z > 1) | ((z == 1) & (onward > 0)))

    def crosses(zp):
        return (beyond(zp) & jnp.logical_not(b_end)) | ((zp == z) & p_helper)

    def a_to_column(zp):
        relayed = q_helper & (zp == end)
        return (crosses(zp) & jnp.logical_not(relayed)) | ((zp == z) & a_end)

    def b_to_column(zp):
        return has_b(zp) & jnp.logical_not(helper & (zp == end))

    def has_b_far(zp):
        return (zp == z) | jnp.logical_not(b_end)

    def has_f(zp):
        return (short(zp) & jnp.logical_not(a_end)) | ((zp == z) & q_helper)

    def has_x(zp):
        return (zp == z) | jnp.logical_not(a_end)

    size = rows // PARTS

    def transfer(send, source, target, zp, device, part):
        here = pl.ds(part * size, size)
        return pltpu.make_async_remote_copy(
            src_ref=held.at[slot(source, zp), here],
            dst_ref=held.at[slot(target, zp), here],
            send_sem=send_sem.at[send * deep + zp, part],
            recv_sem=recv_sem.at[slot(target, zp), part],
            device_id=device,
            device_id_type=MESH,
        )

    def arrived(kind, zp, part):
        transfer(A_UP, kind, kind, zp, sibling, part).wait_recv()

    def sent(send, zp):
        for part in range(PARTS):
            transfer(send, A_NEAR, A_NEAR, zp, sibling, part).wait_send()

    def unit(ref):
        raw = ref[...].astype(jnp.float32)
        inverse = lax.rsqrt(jnp.sum(raw * raw, axis=-1, keepdims=True) + 1e-06)
        return raw * inverse, inverse

    @pl.when(core == 0)
    def _():
        held[slot(A_NEAR, z)] = unit(txt_ref)[0].astype(jnp.bfloat16)
        held[slot(B_NEAR, z)] = unit(img_ref)[0].astype(jnp.bfloat16)

    @pl.when(core == 1)
    def _():
        held[slot(A_NEAR, z)] = unit(img_ref)[0].astype(jnp.bfloat16)
        held[slot(B_NEAR, z)] = unit(txt_ref)[0].astype(jnp.bfloat16)

    barrier = pltpu.get_barrier_semaphore()
    for device in (sibling, after_same, before_same, before_other):
        pl.semaphore_signal(barrier, inc=1, device_id=device, device_id_type=MESH)

    @pl.when(z < deep - 1)
    def _():
        pl.semaphore_signal(barrier, inc=1, device_id=above, device_id_type=MESH)

    @pl.when(z > 0)
    def _():
        pl.semaphore_signal(barrier, inc=1, device_id=below, device_id_type=MESH)

    total[...] = jnp.zeros_like(total)
    losses[...] = jnp.zeros_like(losses)
    edges = jnp.where(z > 0, 1, 0) + jnp.where(z < deep - 1, 1, 0)
    pl.semaphore_wait(barrier, 4 + edges)

    def pass_b(zp, distance, part):
        @pl.when(has_b(zp) & (distance > 0))
        def _():
            arrived(B_NEAR, zp, part)

        @pl.when(b_goes_up(zp))
        def _():
            transfer(B_UP, B_NEAR, B_NEAR, zp, above, part).start()

        @pl.when(b_goes_down(zp))
        def _():
            transfer(B_DOWN, B_NEAR, B_NEAR, zp, below, part).start()

        @pl.when(b_to_column(zp))
        def _():
            transfer(B_COLUMN, B_NEAR, B_FAR, zp, before_other, part).start()

    def pass_a(zp, distance, part):
        @pl.when(has_a(zp) & (distance > 0))
        def _():
            arrived(A_NEAR, zp, part)

        @pl.when(a_goes_up(zp))
        def _():
            transfer(A_UP, A_NEAR, A_NEAR, zp, above, part).start()

        @pl.when(a_goes_down(zp))
        def _():
            transfer(A_DOWN, A_NEAR, A_NEAR, zp, below, part).start()

        @pl.when(a_to_column(zp))
        def _():
            transfer(A_COLUMN, A_NEAR, A_FAR, zp, after_same, part).start()

        @pl.when(has_a(zp))
        def _():
            transfer(A_CORE, A_NEAR, X_NEAR, zp, sibling, part).start()

    def relay():
        for part in range(PARTS):
            arrived(B_FAR, z, part)
            transfer(B_RELAY, B_FAR, B_FAR, z, inner, part).start()

            @pl.when(a_end)
            def _():
                arrived(A_FAR, z, part)
                transfer(A_RELAY, A_FAR, A_FAR, z, inner, part).start()

    def sum_copy():
        return pltpu.make_async_remote_copy(
            src_ref=sums.at[0],
            dst_ref=sums.at[1],
            send_sem=sum_sem.at[0],
            recv_sem=sum_sem.at[1],
            device_id=outer,
            device_id_type=MESH,
        )

    def loss_copy():
        return pltpu.make_async_remote_copy(
            src_ref=losses.at[2],
            dst_ref=loss_in,
            send_sem=sum_sem.at[2],
            recv_sem=sum_sem.at[3],
            device_id=outer,
            device_id_type=MESH,
        )

    diagonal = lax.broadcasted_iota(jnp.int32, (rows, rows), 0) == lax.broadcasted_iota(
        jnp.int32, (rows, rows), 1
    )

    def meet(role, own, other, same):
        logits = (
            scale
            * lax.dot_general(
                held[own],
                held[other],
                (((1,), (1,)), ((), ())),
                preferred_element_type=jnp.float32,
            )
            + offset
        )
        sign = jnp.where(diagonal & same, -1.0, 1.0)
        turned = sign * logits
        small = jnp.exp(-jnp.abs(turned))
        loss = jnp.maximum(turned, 0.0) + jnp.log1p(small)
        sigmoid = jnp.where(turned >= 0.0, 1.0, small) / (1.0 + small)
        weights = (sign * sigmoid * scale).astype(jnp.bfloat16)
        part = loss[:, :LANES]
        for at in range(LANES, rows, LANES):
            part = part + loss[:, at : at + LANES]
        losses[role] += part
        step = 384 if width % 384 == 0 else width
        for at in range(0, width, step):
            total[role, :, at : at + step] += jnp.dot(
                weights, held[other, :, at : at + step], preferred_element_type=jnp.float32
            )

    own_a, own_b = slot(A_NEAR, z), slot(B_NEAR, z)

    def near(zp):
        first = jnp.where(short(zp), 0, jnp.where(beyond(zp), 1, 0))

        def tile(which, carry):
            @pl.when((which == 2) & has_x(zp))
            def _():
                for part in range(PARTS):
                    arrived(X_NEAR, zp, part)

            role = jnp.where(which == 0, 0, 1)
            kind = jnp.where(which == 0, A_NEAR, jnp.where(which == 1, B_NEAR, X_NEAR))
            own = jnp.where(which == 0, own_b, own_a)

            @pl.when(((which == 2) & has_x(zp)) | (which == first) | (zp == z))
            def _():
                meet(role, own, slot(kind, zp), (which < 2) & (zp == z))

            return carry

        lax.fori_loop(0, 3, tile, 0)

    def far(zp):
        @pl.when(has_b_far(zp))
        def _():
            for part in range(PARTS):

                @pl.when(jnp.logical_not(at_end & (zp == z)))
                def _():
                    arrived(B_FAR, zp, part)

                @pl.when(crosses(zp))
                def _():
                    transfer(F_CORE, B_FAR, F_FAR, zp, sibling, part).start()

        helps = helper & (zp != end)

        def tile(which, carry):
            for part in range(PARTS):

                @pl.when((which == 1) & crosses(zp))
                def _():
                    arrived(A_FAR, zp, part)

                @pl.when((which == 1) & has_f(zp))
                def _():
                    arrived(F_FAR, zp, part)

            helping = which < 2
            kind_0 = jnp.where(q_helper, X_NEAR, B_FAR)
            kind_1 = jnp.where(q_helper, F_FAR, A_FAR)
            kind_3 = jnp.where(short(zp), F_FAR, A_FAR)
            kind = jnp.where(
                which == 0,
                kind_0,
                jnp.where(which == 1, kind_1, jnp.where(which == 2, B_FAR, kind_3)),
            )
            in_q = (which == 3) & short(zp)
            own_end = jnp.where(q_helper, slot(A_NEAR, end), slot(B_NEAR, end))
            own = jnp.where(helping, own_end, jnp.where(in_q, own_a, own_b))
            role = jnp.where(helping, 2, jnp.where(in_q, 1, 0))
            other = (zp != z) & jnp.logical_not(at_end)

            @pl.when(
                (helping & helps)
                | ((which == 2) & has_b_far(zp))
                | ((which == 3) & other)
            )
            def _():
                meet(role, own, slot(kind, zp), False)

            @pl.when((which == 1) & helper & (zp == last))
            def _():
                sums[0] = total[2].astype(jnp.bfloat16)
                sum_copy().start()
                loss_copy().start()

            return carry

        lax.fori_loop(0, 4, tile, 0)

    def both_ways(distance, action):
        @pl.when((distance >= 0) & (distance < deep) & (z - distance >= 0))
        def _():
            action(z - distance)

        @pl.when((distance > 0) & (z + distance < deep))
        def _():
            action(z + distance)

    def turn(distance, carry):
        for step in (pass_b, pass_a):
            for part in range(PARTS):
                both_ways(distance, functools.partial(step, distance=distance, part=part))
        both_ways(distance, near)
        pl.when((distance == 0) & at_end)(relay)
        both_ways(distance - 1, far)
        return carry

    lax.fori_loop(0, deep + 1, turn, 0)

    @pl.when(at_end)
    def _():
        sum_copy().wait_recv()
        loss_copy().wait_recv()
        role = jnp.where(a_end, 1, 0)
        total[role] += sums[1].astype(jnp.float32)
        losses[role] += loss_in[...]

    def finish(ref, role):
        unit32, inverse = unit(ref)
        grad = total[role]
        along = jnp.sum(unit32 * grad, axis=-1, keepdims=True)
        return inverse * (grad - unit32 * along)

    grad_img_ref[...] = finish(img_ref, core)
    grad_txt_ref[...] = finish(txt_ref, 1 - core)
    loss_ref[...] = jnp.sum(losses[core], axis=-1, keepdims=True)

    def settle(zp, carry):
        for went, send in (
            (a_goes_up(zp), A_UP),
            (a_goes_down(zp), A_DOWN),
            (b_goes_up(zp), B_UP),
            (b_goes_down(zp), B_DOWN),
            (has_a(zp), A_CORE),
            (a_to_column(zp), A_COLUMN),
            (b_to_column(zp), B_COLUMN),
            (crosses(zp), F_CORE),
            ((zp == z) & a_end, A_RELAY),
            ((zp == z) & at_end, B_RELAY),
        ):
            pl.when(went)(functools.partial(sent, send, zp))
        return carry

    lax.fori_loop(0, deep, settle, 0)

    @pl.when(helper)
    def _():
        sum_copy().wait_send()
        loss_copy().wait_send()


def on_column(columns, deep, images, texts, scale, offset):
    rows, width = images.shape
    tiles = 4 * deep
    loss, grad_images, grad_texts = pl.pallas_call(
        functools.partial(column_kernel, columns, deep),
        out_shape=(
            jax.ShapeDtypeStruct((rows, 1), jnp.float32),
            jax.ShapeDtypeStruct((rows, width), jnp.float32),
            jax.ShapeDtypeStruct((rows, width), jnp.float32),
        ),
        in_specs=[pl.BlockSpec(memory_space=pltpu.SMEM)] * 2
        + [pl.BlockSpec(memory_space=pltpu.VMEM)] * 2,
        out_specs=[pl.BlockSpec(memory_space=pltpu.VMEM)] * 3,
        scratch_shapes=[
            pltpu.VMEM((KINDS * deep, rows, width), jnp.bfloat16),
            pltpu.VMEM((3, rows, width), jnp.float32),
            pltpu.VMEM((3, rows, LANES), jnp.float32),
            pltpu.VMEM((2, rows, width), jnp.bfloat16),
            pltpu.VMEM((rows, LANES), jnp.float32),
            pltpu.SemaphoreType.DMA((SENDS * deep, PARTS)),
            pltpu.SemaphoreType.DMA((KINDS * deep, PARTS)),
            pltpu.SemaphoreType.DMA((4,)),
        ],
        compiler_params=pltpu.CompilerParams(
            collective_id=0, has_side_effects=True, vmem_limit_bytes=48 * 1024 * 1024
        ),
        cost_estimate=pl.CostEstimate(
            flops=tiles * 4 * rows * rows * width,
            bytes_accessed=12 * rows * width,
            transcendentals=tiles * 3 * rows * rows,
        ),
        name="column",
    )(scale, offset, images, texts)
    return loss.reshape(rows), grad_images, grad_texts


def solution(mesh):
    blocks, deep = mesh.shape["blk"], mesh.shape["grp"]
    body = on_device
    if KSTEPS == 2 * deep and deep >= 4 and blocks % 2 == 0 and blocks >= 6:
        body = functools.partial(on_column, blocks // 2, deep)
    return jax.shard_map(
        body,
        mesh=mesh,
        in_specs=(P(("blk", "grp"), None), P(("blk", "grp"), None), P(), P()),
        out_specs=(P(("blk", "grp")), P(("blk", "grp"), None), P(("blk", "grp"), None)),
        check_vma=False,
    )
```

```python
import functools

import jax
import jax.numpy as jnp
from jax import lax
from jax.experimental import pallas as pl
from jax.experimental.pallas import tpu as pltpu
from jax.sharding import PartitionSpec as P

KSTEPS = 8


def passed_along(block, axis, distance):
    devices = range(lax.axis_size(axis))
    route = [((i - distance) % len(devices), i) for i in devices]
    return lax.ppermute(block, axis, route)


def normalize(raw):
    computed_quantities = raw.astype(jnp.float32)
    inverse = lax.rsqrt(
        jnp.sum(computed_quantities * computed_quantities, axis=-1, keepdims=True) + 1e-06
    )
    return (computed_quantities * inverse, inverse)


def back_norm(unit32, inverse, grad_unit):
    along = jnp.sum(unit32 * grad_unit, axis=-1, keepdims=True)
    return inverse * (grad_unit - unit32 * along)


def pairwise_loss_terms(
    image_block_rows, text_block_rows, target_labels, smoothing_coefficient, block_displacement
):
    pair_logit_matrix = (
        smoothing_coefficient
        * lax.dot_general(
            image_block_rows,
            text_block_rows,
            (((1,), (1,)), ((), ())),
            preferred_element_type=jnp.float32,
        )
        + block_displacement
    )
    row_portion = jnp.sum(jax.nn.softplus(-target_labels * pair_logit_matrix), axis=-1)
    sigmoid_weights = (
        -target_labels * jax.nn.sigmoid(-target_labels * pair_logit_matrix) * smoothing_coefficient
    ).astype(jnp.bfloat16)
    return (row_portion, sigmoid_weights)


def image_side(sigmoid_weights, text_block_rows):
    return jnp.dot(sigmoid_weights, text_block_rows, preferred_element_type=jnp.float32)


def text_side(sigmoid_weights, image_block_rows):
    return lax.dot_general(
        sigmoid_weights,
        image_block_rows,
        (((0,), (0,)), ((), ())),
        preferred_element_type=jnp.float32,
    )


def on_device(picture_embedding_array, caption_embedding_array, sharpness_multiplier, score_offset):
    smoothing_coefficient = sharpness_multiplier[0]
    block_displacement = score_offset[0]
    rows = picture_embedding_array.shape[0]
    img_unit32, img_inverse = normalize(picture_embedding_array)
    txt_unit32, txt_inverse = normalize(caption_embedding_array)
    image_unit_vectors = img_unit32.astype(jnp.bfloat16)
    text_unit_vectors = txt_unit32.astype(jnp.bfloat16)
    positions = lax.broadcasted_iota(jnp.int32, (rows, rows), 0)
    columns = lax.broadcasted_iota(jnp.int32, (rows, rows), 1)
    initial_label_values = jnp.where(positions == columns, 1.0, -1.0).astype(jnp.float32)
    negative_labels = jnp.full((rows, rows), -1.0, jnp.float32)
    row_total_sum, sigmoid_weights = pairwise_loss_terms(
        image_unit_vectors,
        text_unit_vectors,
        initial_label_values,
        smoothing_coefficient,
        block_displacement,
    )
    grad_img = image_side(sigmoid_weights, text_unit_vectors)
    own_text = text_side(sigmoid_weights, image_unit_vectors)
    incoming_caption_groups = text_unit_vectors
    carried = own_text
    for hop_index in range(1, KSTEPS):
        incoming_caption_groups, carried = (
            passed_along(incoming_caption_groups, ("blk", "grp"), 1),
            passed_along(carried.astype(jnp.bfloat16), ("blk", "grp"), 1).astype(carried.dtype),
        )
        row_portion, sigmoid_weights = pairwise_loss_terms(
            image_unit_vectors,
            incoming_caption_groups,
            negative_labels,
            smoothing_coefficient,
            block_displacement,
        )
        row_total_sum = row_total_sum + row_portion
        grad_img = grad_img + image_side(sigmoid_weights, incoming_caption_groups)
        carried = carried + text_side(sigmoid_weights, image_unit_vectors)
    grad_txt = passed_along(carried.astype(jnp.bfloat16), ("blk", "grp"), 1 - KSTEPS).astype(
        carried.dtype
    )
    grad_images = back_norm(img_unit32, img_inverse, grad_img)
    grad_texts = back_norm(txt_unit32, txt_inverse, grad_txt)
    return (row_total_sum, grad_images, grad_texts)


MESH = pl.DeviceIdType.MESH
A_NEAR, B_NEAR, X_NEAR, A_FAR, B_FAR, F_FAR = range(6)
KINDS = 6
A_UP, A_DOWN, B_UP, B_DOWN, A_CORE, A_COLUMN, B_COLUMN, F_CORE, A_RELAY, B_RELAY = range(10)
SENDS = 10
LANES = 128
LOG2E = 1.4426950408889634
PARTS = 2


def column_kernel(
    columns,
    deep,
    scale_ref,
    offset_ref,
    img_ref,
    txt_ref,
    loss_ref,
    grad_img_ref,
    grad_txt_ref,
    held,
    total,
    losses,
    sums,
    loss_in,
    send_sem,
    recv_sem,
    sum_sem,
):
    blk = lax.axis_index("blk")
    z = lax.axis_index("grp")
    core = lax.rem(blk, 2)
    column = blk // 2
    onward = 1 - 2 * core
    after = lax.rem(column + onward + columns, columns)
    before = lax.rem(column - onward + columns, columns)
    sibling = (2 * column + 1 - core, z)
    above, below = (blk, z + 1), (blk, z - 1)
    after_same = (2 * after + core, z)
    before_same = (2 * before + core, z)
    before_other = (2 * before + 1 - core, z)
    rows, width = img_ref.shape
    scale, offset = scale_ref[0], offset_ref[0]

    def beyond(zp):
        return (zp - z) * onward > 0

    def short(zp):
        return (zp - z) * onward < 0

    def slot(kind, zp):
        return kind * deep + zp

    at_end = (z == 0) | (z == deep - 1)
    a_end = jnp.where(onward > 0, z == deep - 1, z == 0)
    b_end = jnp.where(onward > 0, z == 0, z == deep - 1)
    q_helper = jnp.where(onward > 0, z == deep - 2, z == 1)
    p_helper = jnp.where(onward > 0, z == 1, z == deep - 2)
    helper = (z == 1) | (z == deep - 2)
    end = jnp.where(z == 1, 0, deep - 1)
    last = deep - 1 - end
    inner = (blk, jnp.where(z == 0, 1, deep - 2))
    outer = (blk, end)

    def has_a(zp):
        return (zp == z) | jnp.logical_not(b_end)

    def has_b(zp):
        return (zp == z) | jnp.logical_not(a_end)

    def a_goes_up(zp):
        return has_a(zp) & (zp <= z) & ((z < deep - 2) | ((z == deep - 2) & (onward > 0)))

    def a_goes_down(zp):
        return has_a(zp) & (zp >= z) & ((z > 1) | ((z == 1) & (onward < 0)))

    def b_goes_up(zp):
        return has_b(zp) & (zp <= z) & ((z < deep - 2) | ((z == deep - 2) & (onward < 0)))

    def b_goes_down(zp):
        return has_b(zp) & (zp >= z) & ((z > 1) | ((z == 1) & (onward > 0)))

    def crosses(zp):
        return (beyond(zp) & jnp.logical_not(b_end)) | ((zp == z) & p_helper)

    def a_to_column(zp):
        relayed = q_helper & (zp == end)
        return (crosses(zp) & jnp.logical_not(relayed)) | ((zp == z) & a_end)

    def b_to_column(zp):
        return has_b(zp) & jnp.logical_not(helper & (zp == end))

    def has_b_far(zp):
        return (zp == z) | jnp.logical_not(b_end)

    def has_f(zp):
        return (short(zp) & jnp.logical_not(a_end)) | ((zp == z) & q_helper)

    def has_x(zp):
        return (zp == z) | jnp.logical_not(a_end)

    size = rows // PARTS

    def transfer(send, source, target, zp, device, part):
        here = pl.ds(part * size, size)
        return pltpu.make_async_remote_copy(
            src_ref=held.at[slot(source, zp), here],
            dst_ref=held.at[slot(target, zp), here],
            send_sem=send_sem.at[send * deep + zp, part],
            recv_sem=recv_sem.at[slot(target, zp), part],
            device_id=device,
            device_id_type=MESH,
        )

    def arrived(kind, zp, part):
        transfer(A_UP, kind, kind, zp, sibling, part).wait_recv()

    def sent(send, zp):
        for part in range(PARTS):
            transfer(send, A_NEAR, A_NEAR, zp, sibling, part).wait_send()

    def unit(ref):
        raw = ref[...].astype(jnp.float32)
        inverse = lax.rsqrt(jnp.sum(raw * raw, axis=-1, keepdims=True) + 1e-06)
        return raw * inverse, inverse

    @pl.when(core == 0)
    def _():
        held[slot(A_NEAR, z)] = unit(txt_ref)[0].astype(jnp.bfloat16)
        held[slot(B_NEAR, z)] = unit(img_ref)[0].astype(jnp.bfloat16)

    @pl.when(core == 1)
    def _():
        held[slot(A_NEAR, z)] = unit(img_ref)[0].astype(jnp.bfloat16)
        held[slot(B_NEAR, z)] = unit(txt_ref)[0].astype(jnp.bfloat16)

    barrier = pltpu.get_barrier_semaphore()
    for device in (sibling, after_same, before_same, before_other):
        pl.semaphore_signal(barrier, inc=1, device_id=device, device_id_type=MESH)

    @pl.when(z < deep - 1)
    def _():
        pl.semaphore_signal(barrier, inc=1, device_id=above, device_id_type=MESH)

    @pl.when(z > 0)
    def _():
        pl.semaphore_signal(barrier, inc=1, device_id=below, device_id_type=MESH)

    total[...] = jnp.zeros_like(total)
    losses[...] = jnp.zeros_like(losses)
    edges = jnp.where(z > 0, 1, 0) + jnp.where(z < deep - 1, 1, 0)
    pl.semaphore_wait(barrier, 4 + edges)

    def pass_b(zp, distance, part):
        @pl.when(has_b(zp) & (distance > 0))
        def _():
            arrived(B_NEAR, zp, part)

        @pl.when(b_goes_up(zp))
        def _():
            transfer(B_UP, B_NEAR, B_NEAR, zp, above, part).start()

        @pl.when(b_goes_down(zp))
        def _():
            transfer(B_DOWN, B_NEAR, B_NEAR, zp, below, part).start()

        @pl.when(b_to_column(zp))
        def _():
            transfer(B_COLUMN, B_NEAR, B_FAR, zp, before_other, part).start()

    def pass_a(zp, distance, part):
        @pl.when(has_a(zp) & (distance > 0))
        def _():
            arrived(A_NEAR, zp, part)

        @pl.when(a_goes_up(zp))
        def _():
            transfer(A_UP, A_NEAR, A_NEAR, zp, above, part).start()

        @pl.when(a_goes_down(zp))
        def _():
            transfer(A_DOWN, A_NEAR, A_NEAR, zp, below, part).start()

        @pl.when(a_to_column(zp))
        def _():
            transfer(A_COLUMN, A_NEAR, A_FAR, zp, after_same, part).start()

        @pl.when(has_a(zp))
        def _():
            transfer(A_CORE, A_NEAR, X_NEAR, zp, sibling, part).start()

    def relay():
        for part in range(PARTS):
            arrived(B_FAR, z, part)
            transfer(B_RELAY, B_FAR, B_FAR, z, inner, part).start()

            @pl.when(a_end)
            def _():
                arrived(A_FAR, z, part)
                transfer(A_RELAY, A_FAR, A_FAR, z, inner, part).start()

    def sum_copy():
        return pltpu.make_async_remote_copy(
            src_ref=sums.at[0],
            dst_ref=sums.at[1],
            send_sem=sum_sem.at[0],
            recv_sem=sum_sem.at[1],
            device_id=outer,
            device_id_type=MESH,
        )

    def loss_copy():
        return pltpu.make_async_remote_copy(
            src_ref=losses.at[2],
            dst_ref=loss_in,
            send_sem=sum_sem.at[2],
            recv_sem=sum_sem.at[3],
            device_id=outer,
            device_id_type=MESH,
        )

    diagonal = lax.broadcasted_iota(jnp.int32, (rows, rows), 0) == lax.broadcasted_iota(
        jnp.int32, (rows, rows), 1
    )

    def weigh(role, own, other, pairs, with_loss):
        dots = lax.dot_general(
            held[own],
            held[other],
            (((1,), (1,)), ((), ())),
            preferred_element_type=jnp.float32,
        )
        if not with_loss:
            power = jnp.exp2(dots * (-LOG2E * scale) - LOG2E * offset)
            return (scale / (1.0 + power)).astype(jnp.bfloat16)
        logits = scale * dots + offset
        turned = jnp.where(diagonal, -logits, logits) if pairs else logits
        small = jnp.exp(-jnp.abs(turned))
        loss = jnp.maximum(turned, 0.0) + jnp.log1p(small)
        part = loss[:, :LANES]
        for at in range(LANES, rows, LANES):
            part = part + loss[:, at : at + LANES]
        losses[role] += part
        weights = jnp.where(turned >= 0.0, scale, scale * small) / (1.0 + small)
        if pairs:
            weights = jnp.where(diagonal, -weights, weights)
        return weights.astype(jnp.bfloat16)

    def meet(role, own, other, pairs):
        def add(with_loss):
            weights = weigh(role, own, other, pairs, with_loss)
            step = 384 if width % 384 == 0 else width
            for at in range(0, width, step):
                total[role, :, at : at + step] += jnp.dot(
                    weights, held[other, :, at : at + step], preferred_element_type=jnp.float32
                )

        if pairs:
            add(True)
            return
        of_image = (role == core) | ((role == 2) & (z == 1))

        @pl.when(of_image)
        def _():
            add(True)

        @pl.when(jnp.logical_not(of_image))
        def _():
            add(False)

    own_a, own_b = slot(A_NEAR, z), slot(B_NEAR, z)

    def near(zp):
        first = jnp.where(short(zp), 0, jnp.where(beyond(zp), 1, 0))

        def tile(which, carry):
            @pl.when((which == 2) & has_x(zp))
            def _():
                for part in range(PARTS):
                    arrived(X_NEAR, zp, part)

            role = jnp.where(which == 0, 0, 1)
            kind = jnp.where(which == 0, A_NEAR, jnp.where(which == 1, B_NEAR, X_NEAR))
            own = jnp.where(which == 0, own_b, own_a)

            @pl.when((which < 2) & (zp == z))
            def _():
                meet(role, own, slot(kind, zp), True)

            @pl.when(((which == 2) & has_x(zp)) | ((which == first) & (zp != z)))
            def _():
                meet(role, own, slot(kind, zp), False)

            return carry

        lax.fori_loop(0, 3, tile, 0)

    def far(zp):
        @pl.when(has_b_far(zp))
        def _():
            for part in range(PARTS):

                @pl.when(jnp.logical_not(at_end & (zp == z)))
                def _():
                    arrived(B_FAR, zp, part)

                @pl.when(crosses(zp))
                def _():
                    transfer(F_CORE, B_FAR, F_FAR, zp, sibling, part).start()

        helps = helper & (zp != end)

        def tile(which, carry):
            for part in range(PARTS):

                @pl.when((which == 1) & crosses(zp))
                def _():
                    arrived(A_FAR, zp, part)

                @pl.when((which == 1) & has_f(zp))
                def _():
                    arrived(F_FAR, zp, part)

            helping = which < 2
            kind_0 = jnp.where(q_helper, X_NEAR, B_FAR)
            kind_1 = jnp.where(q_helper, F_FAR, A_FAR)
            kind_3 = jnp.where(short(zp), F_FAR, A_FAR)
            kind = jnp.where(
                which == 0,
                kind_0,
                jnp.where(which == 1, kind_1, jnp.where(which == 2, B_FAR, kind_3)),
            )
            in_q = (which == 3) & short(zp)
            own_end = jnp.where(q_helper, slot(A_NEAR, end), slot(B_NEAR, end))
            own = jnp.where(helping, own_end, jnp.where(in_q, own_a, own_b))
            role = jnp.where(helping, 2, jnp.where(in_q, 1, 0))
            other = (zp != z) & jnp.logical_not(at_end)

            @pl.when(
                (helping & helps)
                | ((which == 2) & has_b_far(zp))
                | ((which == 3) & other)
            )
            def _():
                meet(role, own, slot(kind, zp), False)

            @pl.when((which == 1) & helper & (zp == last))
            def _():
                sums[0] = total[2].astype(jnp.bfloat16)
                sum_copy().start()
                loss_copy().start()

            return carry

        lax.fori_loop(0, 4, tile, 0)

    def both_ways(distance, action):
        @pl.when((distance >= 0) & (distance < deep) & (z - distance >= 0))
        def _():
            action(z - distance)

        @pl.when((distance > 0) & (z + distance < deep))
        def _():
            action(z + distance)

    def turn(distance, carry):
        for step in (pass_b, pass_a):
            for part in range(PARTS):
                both_ways(distance, functools.partial(step, distance=distance, part=part))
        both_ways(distance, near)
        pl.when((distance == 0) & at_end)(relay)
        both_ways(distance - 1, far)
        return carry

    lax.fori_loop(0, deep + 1, turn, 0)

    @pl.when(at_end)
    def _():
        sum_copy().wait_recv()
        loss_copy().wait_recv()
        role = jnp.where(a_end, 1, 0)
        total[role] += sums[1].astype(jnp.float32)
        losses[role] += loss_in[...]

    def finish(ref, role):
        unit32, inverse = unit(ref)
        grad = total[role]
        along = jnp.sum(unit32 * grad, axis=-1, keepdims=True)
        return inverse * (grad - unit32 * along)

    grad_img_ref[...] = finish(img_ref, core)
    grad_txt_ref[...] = finish(txt_ref, 1 - core)
    loss_ref[...] = jnp.sum(losses[core], axis=-1, keepdims=True)

    def settle(zp, carry):
        for went, send in (
            (a_goes_up(zp), A_UP),
            (a_goes_down(zp), A_DOWN),
            (b_goes_up(zp), B_UP),
            (b_goes_down(zp), B_DOWN),
            (has_a(zp), A_CORE),
            (a_to_column(zp), A_COLUMN),
            (b_to_column(zp), B_COLUMN),
            (crosses(zp), F_CORE),
            ((zp == z) & a_end, A_RELAY),
            ((zp == z) & at_end, B_RELAY),
        ):
            pl.when(went)(functools.partial(sent, send, zp))
        return carry

    lax.fori_loop(0, deep, settle, 0)

    @pl.when(helper)
    def _():
        sum_copy().wait_send()
        loss_copy().wait_send()


def on_column(columns, deep, images, texts, scale, offset):
    rows, width = images.shape
    tiles = 4 * deep
    loss, grad_images, grad_texts = pl.pallas_call(
        functools.partial(column_kernel, columns, deep),
        out_shape=(
            jax.ShapeDtypeStruct((rows, 1), jnp.float32),
            jax.ShapeDtypeStruct((rows, width), jnp.float32),
            jax.ShapeDtypeStruct((rows, width), jnp.float32),
        ),
        in_specs=[pl.BlockSpec(memory_space=pltpu.SMEM)] * 2
        + [pl.BlockSpec(memory_space=pltpu.VMEM)] * 2,
        out_specs=[pl.BlockSpec(memory_space=pltpu.VMEM)] * 3,
        scratch_shapes=[
            pltpu.VMEM((KINDS * deep, rows, width), jnp.bfloat16),
            pltpu.VMEM((3, rows, width), jnp.float32),
            pltpu.VMEM((3, rows, LANES), jnp.float32),
            pltpu.VMEM((2, rows, width), jnp.bfloat16),
            pltpu.VMEM((rows, LANES), jnp.float32),
            pltpu.SemaphoreType.DMA((SENDS * deep, PARTS)),
            pltpu.SemaphoreType.DMA((KINDS * deep, PARTS)),
            pltpu.SemaphoreType.DMA((4,)),
        ],
        compiler_params=pltpu.CompilerParams(
            collective_id=0, has_side_effects=True, vmem_limit_bytes=48 * 1024 * 1024
        ),
        cost_estimate=pl.CostEstimate(
            flops=tiles * 4 * rows * rows * width,
            bytes_accessed=12 * rows * width,
            transcendentals=tiles * 3 * rows * rows,
        ),
        name="column",
    )(scale, offset, images, texts)
    return loss.reshape(rows), grad_images, grad_texts


def solution(mesh):
    blocks, deep = mesh.shape["blk"], mesh.shape["grp"]
    body = on_device
    if KSTEPS == 2 * deep and deep >= 4 and blocks % 2 == 0 and blocks >= 6:
        body = functools.partial(on_column, blocks // 2, deep)
    return jax.shard_map(
        body,
        mesh=mesh,
        in_specs=(P(("blk", "grp"), None), P(("blk", "grp"), None), P(), P()),
        out_specs=(P(("blk", "grp")), P(("blk", "grp"), None), P(("blk", "grp"), None)),
        check_vma=False,
    )
```

```python
import functools

import jax
import jax.numpy as jnp
from jax import lax
from jax.experimental import pallas as pl
from jax.experimental.pallas import tpu as pltpu
from jax.sharding import PartitionSpec as P

KSTEPS = 8


def passed_along(block, axis, distance):
    devices = range(lax.axis_size(axis))
    route = [((i - distance) % len(devices), i) for i in devices]
    return lax.ppermute(block, axis, route)


def normalize(raw):
    computed_quantities = raw.astype(jnp.float32)
    inverse = lax.rsqrt(
        jnp.sum(computed_quantities * computed_quantities, axis=-1, keepdims=True) + 1e-06
    )
    return (computed_quantities * inverse, inverse)


def back_norm(unit32, inverse, grad_unit):
    along = jnp.sum(unit32 * grad_unit, axis=-1, keepdims=True)
    return inverse * (grad_unit - unit32 * along)


def pairwise_loss_terms(
    image_block_rows, text_block_rows, target_labels, smoothing_coefficient, block_displacement
):
    pair_logit_matrix = (
        smoothing_coefficient
        * lax.dot_general(
            image_block_rows,
            text_block_rows,
            (((1,), (1,)), ((), ())),
            preferred_element_type=jnp.float32,
        )
        + block_displacement
    )
    row_portion = jnp.sum(jax.nn.softplus(-target_labels * pair_logit_matrix), axis=-1)
    sigmoid_weights = (
        -target_labels * jax.nn.sigmoid(-target_labels * pair_logit_matrix) * smoothing_coefficient
    ).astype(jnp.bfloat16)
    return (row_portion, sigmoid_weights)


def image_side(sigmoid_weights, text_block_rows):
    return jnp.dot(sigmoid_weights, text_block_rows, preferred_element_type=jnp.float32)


def text_side(sigmoid_weights, image_block_rows):
    return lax.dot_general(
        sigmoid_weights,
        image_block_rows,
        (((0,), (0,)), ((), ())),
        preferred_element_type=jnp.float32,
    )


def on_device(picture_embedding_array, caption_embedding_array, sharpness_multiplier, score_offset):
    smoothing_coefficient = sharpness_multiplier[0]
    block_displacement = score_offset[0]
    rows = picture_embedding_array.shape[0]
    img_unit32, img_inverse = normalize(picture_embedding_array)
    txt_unit32, txt_inverse = normalize(caption_embedding_array)
    image_unit_vectors = img_unit32.astype(jnp.bfloat16)
    text_unit_vectors = txt_unit32.astype(jnp.bfloat16)
    positions = lax.broadcasted_iota(jnp.int32, (rows, rows), 0)
    columns = lax.broadcasted_iota(jnp.int32, (rows, rows), 1)
    initial_label_values = jnp.where(positions == columns, 1.0, -1.0).astype(jnp.float32)
    negative_labels = jnp.full((rows, rows), -1.0, jnp.float32)
    row_total_sum, sigmoid_weights = pairwise_loss_terms(
        image_unit_vectors,
        text_unit_vectors,
        initial_label_values,
        smoothing_coefficient,
        block_displacement,
    )
    grad_img = image_side(sigmoid_weights, text_unit_vectors)
    own_text = text_side(sigmoid_weights, image_unit_vectors)
    incoming_caption_groups = text_unit_vectors
    carried = own_text
    for hop_index in range(1, KSTEPS):
        incoming_caption_groups, carried = (
            passed_along(incoming_caption_groups, ("blk", "grp"), 1),
            passed_along(carried.astype(jnp.bfloat16), ("blk", "grp"), 1).astype(carried.dtype),
        )
        row_portion, sigmoid_weights = pairwise_loss_terms(
            image_unit_vectors,
            incoming_caption_groups,
            negative_labels,
            smoothing_coefficient,
            block_displacement,
        )
        row_total_sum = row_total_sum + row_portion
        grad_img = grad_img + image_side(sigmoid_weights, incoming_caption_groups)
        carried = carried + text_side(sigmoid_weights, image_unit_vectors)
    grad_txt = passed_along(carried.astype(jnp.bfloat16), ("blk", "grp"), 1 - KSTEPS).astype(
        carried.dtype
    )
    grad_images = back_norm(img_unit32, img_inverse, grad_img)
    grad_texts = back_norm(txt_unit32, txt_inverse, grad_txt)
    return (row_total_sum, grad_images, grad_texts)


MESH = pl.DeviceIdType.MESH
A_NEAR, B_NEAR, X_NEAR, A_FAR, B_FAR, F_FAR = range(6)
KINDS = 6
A_UP, A_DOWN, B_UP, B_DOWN, A_CORE, A_COLUMN, B_COLUMN, F_CORE, A_RELAY, B_RELAY = range(10)
SENDS = 10
LANES = 128
LOG2E = 1.4426950408889634
PARTS = 2


def column_kernel(
    columns,
    deep,
    scale_ref,
    offset_ref,
    img_ref,
    txt_ref,
    loss_ref,
    grad_img_ref,
    grad_txt_ref,
    held,
    total,
    losses,
    sums,
    loss_in,
    send_sem,
    recv_sem,
    sum_sem,
):
    blk = lax.axis_index("blk")
    z = lax.axis_index("grp")
    core = lax.rem(blk, 2)
    column = blk // 2
    onward = 1 - 2 * core
    after = lax.rem(column + onward + columns, columns)
    before = lax.rem(column - onward + columns, columns)
    sibling = (2 * column + 1 - core, z)
    above, below = (blk, z + 1), (blk, z - 1)
    after_same = (2 * after + core, z)
    before_same = (2 * before + core, z)
    before_other = (2 * before + 1 - core, z)
    rows, width = img_ref.shape
    scale, offset = scale_ref[0], offset_ref[0]

    def beyond(zp):
        return (zp - z) * onward > 0

    def short(zp):
        return (zp - z) * onward < 0

    def slot(kind, zp):
        return kind * deep + zp

    at_end = (z == 0) | (z == deep - 1)
    a_end = jnp.where(onward > 0, z == deep - 1, z == 0)
    b_end = jnp.where(onward > 0, z == 0, z == deep - 1)
    q_helper = jnp.where(onward > 0, z == deep - 2, z == 1)
    p_helper = jnp.where(onward > 0, z == 1, z == deep - 2)
    helper = (z == 1) | (z == deep - 2)
    end = jnp.where(z == 1, 0, deep - 1)
    last = deep - 1 - end
    inner = (blk, jnp.where(z == 0, 1, deep - 2))
    outer = (blk, end)

    final = jnp.where(end == 0, deep - 2, 1)

    def through(zp):
        return (zp == z) | (zp == deep - 1 - z)

    def has_a(zp):
        return through(zp) | jnp.logical_not(b_end)

    def has_b(zp):
        return through(zp) | jnp.logical_not(a_end)

    def a_goes_up(zp):
        return has_a(zp) & (zp <= z) & ((z < deep - 2) | ((z == deep - 2) & ((onward > 0) | (zp == 0))))

    def a_goes_down(zp):
        return has_a(zp) & (zp >= z) & ((z > 1) | ((z == 1) & ((onward < 0) | (zp == deep - 1))))

    def b_goes_up(zp):
        return has_b(zp) & (zp <= z) & ((z < deep - 2) | ((z == deep - 2) & ((onward < 0) | (zp == 0))))

    def b_goes_down(zp):
        return has_b(zp) & (zp >= z) & ((z > 1) | ((z == 1) & ((onward > 0) | (zp == deep - 1))))

    def crosses(zp):
        return (beyond(zp) & (through(zp) | jnp.logical_not(b_end))) | ((zp == z) & p_helper)

    def a_to_column(zp):
        relayed = q_helper & (zp == end)
        return (crosses(zp) & jnp.logical_not(relayed)) | ((zp == z) & a_end)

    def b_to_column(zp):
        return has_b(zp) & jnp.logical_not(helper & (zp == end))

    def has_b_far(zp):
        return through(zp) | jnp.logical_not(b_end)

    def has_f(zp):
        return (short(zp) & (through(zp) | jnp.logical_not(a_end))) | ((zp == z) & q_helper)

    def has_x(zp):
        return through(zp) | jnp.logical_not(a_end)

    size = rows // PARTS

    def transfer(send, source, target, zp, device, part):
        here = pl.ds(part * size, size)
        return pltpu.make_async_remote_copy(
            src_ref=held.at[slot(source, zp), here],
            dst_ref=held.at[slot(target, zp), here],
            send_sem=send_sem.at[send * deep + zp, part],
            recv_sem=recv_sem.at[slot(target, zp), part],
            device_id=device,
            device_id_type=MESH,
        )

    def arrived(kind, zp, part):
        transfer(A_UP, kind, kind, zp, sibling, part).wait_recv()

    def sent(send, zp):
        for part in range(PARTS):
            transfer(send, A_NEAR, A_NEAR, zp, sibling, part).wait_send()

    def unit(ref):
        raw = ref[...].astype(jnp.float32)
        inverse = lax.rsqrt(jnp.sum(raw * raw, axis=-1, keepdims=True) + 1e-06)
        return raw * inverse, inverse

    @pl.when(core == 0)
    def _():
        held[slot(A_NEAR, z)] = unit(txt_ref)[0].astype(jnp.bfloat16)
        held[slot(B_NEAR, z)] = unit(img_ref)[0].astype(jnp.bfloat16)

    @pl.when(core == 1)
    def _():
        held[slot(A_NEAR, z)] = unit(img_ref)[0].astype(jnp.bfloat16)
        held[slot(B_NEAR, z)] = unit(txt_ref)[0].astype(jnp.bfloat16)

    barrier = pltpu.get_barrier_semaphore()
    for device in (sibling, after_same, before_same, before_other):
        pl.semaphore_signal(barrier, inc=1, device_id=device, device_id_type=MESH)

    @pl.when(z < deep - 1)
    def _():
        pl.semaphore_signal(barrier, inc=1, device_id=above, device_id_type=MESH)

    @pl.when(z > 0)
    def _():
        pl.semaphore_signal(barrier, inc=1, device_id=below, device_id_type=MESH)

    total[...] = jnp.zeros_like(total)
    losses[...] = jnp.zeros_like(losses)
    edges = jnp.where(z > 0, 1, 0) + jnp.where(z < deep - 1, 1, 0)
    pl.semaphore_wait(barrier, 4 + edges)

    def pass_b(zp, distance, part):
        @pl.when(has_b(zp) & (distance > 0))
        def _():
            arrived(B_NEAR, zp, part)

        @pl.when(b_goes_up(zp))
        def _():
            transfer(B_UP, B_NEAR, B_NEAR, zp, above, part).start()

        @pl.when(b_goes_down(zp))
        def _():
            transfer(B_DOWN, B_NEAR, B_NEAR, zp, below, part).start()

        @pl.when(b_to_column(zp))
        def _():
            transfer(B_COLUMN, B_NEAR, B_FAR, zp, before_other, part).start()

    def pass_a(zp, distance, part):
        @pl.when(has_a(zp) & (distance > 0))
        def _():
            arrived(A_NEAR, zp, part)

        @pl.when(a_goes_up(zp))
        def _():
            transfer(A_UP, A_NEAR, A_NEAR, zp, above, part).start()

        @pl.when(a_goes_down(zp))
        def _():
            transfer(A_DOWN, A_NEAR, A_NEAR, zp, below, part).start()

        @pl.when(a_to_column(zp))
        def _():
            transfer(A_COLUMN, A_NEAR, A_FAR, zp, after_same, part).start()

        @pl.when(has_a(zp))
        def _():
            transfer(A_CORE, A_NEAR, X_NEAR, zp, sibling, part).start()

    def relay():
        for part in range(PARTS):
            arrived(B_FAR, z, part)
            transfer(B_RELAY, B_FAR, B_FAR, z, inner, part).start()

            @pl.when(a_end)
            def _():
                arrived(A_FAR, z, part)
                transfer(A_RELAY, A_FAR, A_FAR, z, inner, part).start()

    def sum_copy():
        return pltpu.make_async_remote_copy(
            src_ref=sums.at[0],
            dst_ref=sums.at[1],
            send_sem=sum_sem.at[0],
            recv_sem=sum_sem.at[1],
            device_id=outer,
            device_id_type=MESH,
        )

    def loss_copy():
        return pltpu.make_async_remote_copy(
            src_ref=losses.at[2],
            dst_ref=loss_in,
            send_sem=sum_sem.at[2],
            recv_sem=sum_sem.at[3],
            device_id=outer,
            device_id_type=MESH,
        )

    diagonal = lax.broadcasted_iota(jnp.int32, (rows, rows), 0) == lax.broadcasted_iota(
        jnp.int32, (rows, rows), 1
    )

    def weigh(role, own, other, pairs, with_loss):
        dots = lax.dot_general(
            held[own],
            held[other],
            (((1,), (1,)), ((), ())),
            preferred_element_type=jnp.float32,
        )
        if not with_loss:
            power = jnp.exp2(dots * (-LOG2E * scale) - LOG2E * offset)
            return (scale / (1.0 + power)).astype(jnp.bfloat16)
        logits = scale * dots + offset
        turned = jnp.where(diagonal, -logits, logits) if pairs else logits
        small = jnp.exp(-jnp.abs(turned))
        loss = jnp.maximum(turned, 0.0) + jnp.log1p(small)
        part = loss[:, :LANES]
        for at in range(LANES, rows, LANES):
            part = part + loss[:, at : at + LANES]
        losses[role] += part
        weights = jnp.where(turned >= 0.0, scale, scale * small) / (1.0 + small)
        if pairs:
            weights = jnp.where(diagonal, -weights, weights)
        return weights.astype(jnp.bfloat16)

    def meet(role, own, other, pairs):
        def add(with_loss):
            weights = weigh(role, own, other, pairs, with_loss)
            step = 384 if width % 384 == 0 else width
            for at in range(0, width, step):
                total[role, :, at : at + step] += jnp.dot(
                    weights, held[other, :, at : at + step], preferred_element_type=jnp.float32
                )

        if pairs:
            add(True)
            return
        of_image = (role == core) | ((role == 2) & (z == 1))

        @pl.when(of_image)
        def _():
            add(True)

        @pl.when(jnp.logical_not(of_image))
        def _():
            add(False)

    own_a, own_b = slot(A_NEAR, z), slot(B_NEAR, z)

    def near(zp):
        first = jnp.where(short(zp), 0, jnp.where(beyond(zp), 1, 0))

        def tile(which, carry):
            @pl.when((which == 2) & has_x(zp))
            def _():
                for part in range(PARTS):
                    arrived(X_NEAR, zp, part)

            role = jnp.where(which == 0, 0, 1)
            kind = jnp.where(which == 0, A_NEAR, jnp.where(which == 1, B_NEAR, X_NEAR))
            own = jnp.where(which == 0, own_b, own_a)

            @pl.when((which < 2) & (zp == z))
            def _():
                meet(role, own, slot(kind, zp), True)

            @pl.when(((which == 2) & has_x(zp)) | ((which == first) & (zp != z)))
            def _():
                meet(role, own, slot(kind, zp), False)

            return carry

        lax.fori_loop(0, 3, tile, 0)

    def far(zp):
        @pl.when(has_b_far(zp))
        def _():
            for part in range(PARTS):

                @pl.when(jnp.logical_not(at_end & (zp == z)))
                def _():
                    arrived(B_FAR, zp, part)

                @pl.when(crosses(zp))
                def _():
                    transfer(F_CORE, B_FAR, F_FAR, zp, sibling, part).start()

        helps = helper & (zp != end) & (zp != last)

        def tile(which, carry):
            for part in range(PARTS):

                @pl.when((which == 1) & crosses(zp))
                def _():
                    arrived(A_FAR, zp, part)

                @pl.when((which == 1) & has_f(zp))
                def _():
                    arrived(F_FAR, zp, part)

            helping = which < 2
            kind_0 = jnp.where(q_helper, X_NEAR, B_FAR)
            kind_1 = jnp.where(q_helper, F_FAR, A_FAR)
            kind_3 = jnp.where(short(zp), F_FAR, A_FAR)
            kind = jnp.where(
                which == 0,
                kind_0,
                jnp.where(which == 1, kind_1, jnp.where(which == 2, B_FAR, kind_3)),
            )
            in_q = (which == 3) & short(zp)
            own_end = jnp.where(q_helper, slot(A_NEAR, end), slot(B_NEAR, end))
            own = jnp.where(helping, own_end, jnp.where(in_q, own_a, own_b))
            role = jnp.where(helping, 2, jnp.where(in_q, 1, 0))
            other = (zp != z) & (through(zp) | jnp.logical_not(at_end))

            @pl.when(
                (helping & helps)
                | ((which == 2) & has_b_far(zp))
                | ((which == 3) & other)
            )
            def _():
                meet(role, own, slot(kind, zp), False)

            @pl.when((which == 1) & helper & (zp == final))
            def _():
                sums[0] = total[2].astype(jnp.bfloat16)
                sum_copy().start()

                @pl.when(z == 1)
                def _():
                    loss_copy().start()

            return carry

        lax.fori_loop(0, 4, tile, 0)

    inward = jnp.where(z < deep // 2, 1, -1)

    def both_ways(distance, action):
        ahead, behind = z + inward * distance, z - inward * distance

        @pl.when((distance >= 0) & (distance < deep) & (ahead >= 0) & (ahead < deep))
        def _():
            action(ahead)

        @pl.when((distance > 0) & (behind >= 0) & (behind < deep))
        def _():
            action(behind)

    def turn(distance, carry):
        for step in (pass_b, pass_a):
            for part in range(PARTS):
                both_ways(distance, functools.partial(step, distance=distance, part=part))
        both_ways(distance, near)
        pl.when((distance == 0) & at_end)(relay)
        both_ways(distance - 1, far)
        return carry

    lax.fori_loop(0, deep + 1, turn, 0)

    @pl.when(at_end)
    def _():
        sum_copy().wait_recv()
        role = jnp.where(a_end, 1, 0)
        total[role] += sums[1].astype(jnp.float32)

        @pl.when(z == 0)
        def _():
            loss_copy().wait_recv()
            losses[role] += loss_in[...]

    def finish(ref, role):
        unit32, inverse = unit(ref)
        grad = total[role]
        along = jnp.sum(unit32 * grad, axis=-1, keepdims=True)
        return inverse * (grad - unit32 * along)

    grad_img_ref[...] = finish(img_ref, core)
    grad_txt_ref[...] = finish(txt_ref, 1 - core)
    loss_ref[...] = jnp.sum(losses[core], axis=-1, keepdims=True)

    def settle(zp, carry):
        for went, send in (
            (a_goes_up(zp), A_UP),
            (a_goes_down(zp), A_DOWN),
            (b_goes_up(zp), B_UP),
            (b_goes_down(zp), B_DOWN),
            (has_a(zp), A_CORE),
            (a_to_column(zp), A_COLUMN),
            (b_to_column(zp), B_COLUMN),
            (crosses(zp), F_CORE),
            ((zp == z) & a_end, A_RELAY),
            ((zp == z) & at_end, B_RELAY),
        ):
            pl.when(went)(functools.partial(sent, send, zp))
        return carry

    lax.fori_loop(0, deep, settle, 0)

    @pl.when(helper)
    def _():
        sum_copy().wait_send()
        pl.when(z == 1)(lambda: loss_copy().wait_send())


def on_column(columns, deep, images, texts, scale, offset):
    rows, width = images.shape
    tiles = 4 * deep
    loss, grad_images, grad_texts = pl.pallas_call(
        functools.partial(column_kernel, columns, deep),
        out_shape=(
            jax.ShapeDtypeStruct((rows, 1), jnp.float32),
            jax.ShapeDtypeStruct((rows, width), jnp.float32),
            jax.ShapeDtypeStruct((rows, width), jnp.float32),
        ),
        in_specs=[pl.BlockSpec(memory_space=pltpu.SMEM)] * 2
        + [pl.BlockSpec(memory_space=pltpu.VMEM)] * 2,
        out_specs=[pl.BlockSpec(memory_space=pltpu.VMEM)] * 3,
        scratch_shapes=[
            pltpu.VMEM((KINDS * deep, rows, width), jnp.bfloat16),
            pltpu.VMEM((3, rows, width), jnp.float32),
            pltpu.VMEM((3, rows, LANES), jnp.float32),
            pltpu.VMEM((2, rows, width), jnp.bfloat16),
            pltpu.VMEM((rows, LANES), jnp.float32),
            pltpu.SemaphoreType.DMA((SENDS * deep, PARTS)),
            pltpu.SemaphoreType.DMA((KINDS * deep, PARTS)),
            pltpu.SemaphoreType.DMA((4,)),
        ],
        compiler_params=pltpu.CompilerParams(
            collective_id=0, has_side_effects=True, vmem_limit_bytes=48 * 1024 * 1024
        ),
        cost_estimate=pl.CostEstimate(
            flops=tiles * 4 * rows * rows * width,
            bytes_accessed=12 * rows * width,
            transcendentals=tiles * 3 * rows * rows,
        ),
        name="column",
    )(scale, offset, images, texts)
    return loss.reshape(rows), grad_images, grad_texts


def solution(mesh):
    blocks, deep = mesh.shape["blk"], mesh.shape["grp"]
    body = on_device
    if KSTEPS == 2 * deep and deep >= 4 and blocks % 2 == 0 and blocks >= 6:
        body = functools.partial(on_column, blocks // 2, deep)
    return jax.shard_map(
        body,
        mesh=mesh,
        in_specs=(P(("blk", "grp"), None), P(("blk", "grp"), None), P(), P()),
        out_specs=(P(("blk", "grp")), P(("blk", "grp"), None), P(("blk", "grp"), None)),
        check_vma=False,
    )
```

```python
import functools

import jax
import jax.numpy as jnp
from jax import lax
from jax.experimental import pallas as pl
from jax.experimental.pallas import tpu as pltpu
from jax.sharding import PartitionSpec as P

KSTEPS = 8


def passed_along(block, axis, distance):
    devices = range(lax.axis_size(axis))
    route = [((i - distance) % len(devices), i) for i in devices]
    return lax.ppermute(block, axis, route)


def normalize(raw):
    computed_quantities = raw.astype(jnp.float32)
    inverse = lax.rsqrt(
        jnp.sum(computed_quantities * computed_quantities, axis=-1, keepdims=True) + 1e-06
    )
    return (computed_quantities * inverse, inverse)


def back_norm(unit32, inverse, grad_unit):
    along = jnp.sum(unit32 * grad_unit, axis=-1, keepdims=True)
    return inverse * (grad_unit - unit32 * along)


def pairwise_loss_terms(
    image_block_rows, text_block_rows, target_labels, smoothing_coefficient, block_displacement
):
    pair_logit_matrix = (
        smoothing_coefficient
        * lax.dot_general(
            image_block_rows,
            text_block_rows,
            (((1,), (1,)), ((), ())),
            preferred_element_type=jnp.float32,
        )
        + block_displacement
    )
    row_portion = jnp.sum(jax.nn.softplus(-target_labels * pair_logit_matrix), axis=-1)
    sigmoid_weights = (
        -target_labels * jax.nn.sigmoid(-target_labels * pair_logit_matrix) * smoothing_coefficient
    ).astype(jnp.bfloat16)
    return (row_portion, sigmoid_weights)


def image_side(sigmoid_weights, text_block_rows):
    return jnp.dot(sigmoid_weights, text_block_rows, preferred_element_type=jnp.float32)


def text_side(sigmoid_weights, image_block_rows):
    return lax.dot_general(
        sigmoid_weights,
        image_block_rows,
        (((0,), (0,)), ((), ())),
        preferred_element_type=jnp.float32,
    )


def on_device(picture_embedding_array, caption_embedding_array, sharpness_multiplier, score_offset):
    smoothing_coefficient = sharpness_multiplier[0]
    block_displacement = score_offset[0]
    rows = picture_embedding_array.shape[0]
    img_unit32, img_inverse = normalize(picture_embedding_array)
    txt_unit32, txt_inverse = normalize(caption_embedding_array)
    image_unit_vectors = img_unit32.astype(jnp.bfloat16)
    text_unit_vectors = txt_unit32.astype(jnp.bfloat16)
    positions = lax.broadcasted_iota(jnp.int32, (rows, rows), 0)
    columns = lax.broadcasted_iota(jnp.int32, (rows, rows), 1)
    initial_label_values = jnp.where(positions == columns, 1.0, -1.0).astype(jnp.float32)
    negative_labels = jnp.full((rows, rows), -1.0, jnp.float32)
    row_total_sum, sigmoid_weights = pairwise_loss_terms(
        image_unit_vectors,
        text_unit_vectors,
        initial_label_values,
        smoothing_coefficient,
        block_displacement,
    )
    grad_img = image_side(sigmoid_weights, text_unit_vectors)
    own_text = text_side(sigmoid_weights, image_unit_vectors)
    incoming_caption_groups = text_unit_vectors
    carried = own_text
    for hop_index in range(1, KSTEPS):
        incoming_caption_groups, carried = (
            passed_along(incoming_caption_groups, ("blk", "grp"), 1),
            passed_along(carried.astype(jnp.bfloat16), ("blk", "grp"), 1).astype(carried.dtype),
        )
        row_portion, sigmoid_weights = pairwise_loss_terms(
            image_unit_vectors,
            incoming_caption_groups,
            negative_labels,
            smoothing_coefficient,
            block_displacement,
        )
        row_total_sum = row_total_sum + row_portion
        grad_img = grad_img + image_side(sigmoid_weights, incoming_caption_groups)
        carried = carried + text_side(sigmoid_weights, image_unit_vectors)
    grad_txt = passed_along(carried.astype(jnp.bfloat16), ("blk", "grp"), 1 - KSTEPS).astype(
        carried.dtype
    )
    grad_images = back_norm(img_unit32, img_inverse, grad_img)
    grad_texts = back_norm(txt_unit32, txt_inverse, grad_txt)
    return (row_total_sum, grad_images, grad_texts)


MESH = pl.DeviceIdType.MESH
A_NEAR, B_NEAR, X_NEAR, A_FAR, B_FAR, F_FAR = range(6)
KINDS = 6
A_UP, A_DOWN, B_UP, B_DOWN, A_CORE, A_COLUMN, B_COLUMN, F_CORE, A_RELAY, B_RELAY = range(10)
SENDS = 10
LANES = 128
LOG2E = 1.4426950408889634
PARTS = 2


def column_kernel(
    columns,
    deep,
    scale_ref,
    offset_ref,
    img_hbm,
    txt_hbm,
    loss_ref,
    grad_img_ref,
    grad_txt_ref,
    held,
    total,
    losses,
    sums,
    loss_row,
    raw,
    raw_sem,
    send_sem,
    recv_sem,
    sum_sem,
):
    blk = lax.axis_index("blk")
    z = lax.axis_index("grp")
    core = lax.rem(blk, 2)
    column = blk // 2
    onward = 1 - 2 * core
    after = lax.rem(column + onward + columns, columns)
    before = lax.rem(column - onward + columns, columns)
    sibling = (2 * column + 1 - core, z)
    above, below = (blk, z + 1), (blk, z - 1)
    after_same = (2 * after + core, z)
    before_same = (2 * before + core, z)
    before_other = (2 * before + 1 - core, z)
    rows, width = img_hbm.shape
    copies = [
        pltpu.make_async_copy(source, raw.at[at], raw_sem.at[at])
        for at, source in enumerate((img_hbm, txt_hbm))
    ]
    for copy in copies:
        copy.start()
    scale, offset = scale_ref[0], offset_ref[0]

    def beyond(zp):
        return (zp - z) * onward > 0

    def short(zp):
        return (zp - z) * onward < 0

    def slot(kind, zp):
        return kind * deep + zp

    at_end = (z == 0) | (z == deep - 1)
    a_end = jnp.where(onward > 0, z == deep - 1, z == 0)
    b_end = jnp.where(onward > 0, z == 0, z == deep - 1)
    q_helper = jnp.where(onward > 0, z == deep - 2, z == 1)
    p_helper = jnp.where(onward > 0, z == 1, z == deep - 2)
    helper = (z == 1) | (z == deep - 2)
    end = jnp.where(z == 1, 0, deep - 1)
    last = deep - 1 - end
    inner = (blk, jnp.where(z == 0, 1, deep - 2))
    outer = (blk, end)

    final = jnp.where(end == 0, deep - 2, 1)

    def through(zp):
        return (zp == z) | (zp == deep - 1 - z)

    def has_a(zp):
        return through(zp) | jnp.logical_not(b_end)

    def has_b(zp):
        return through(zp) | jnp.logical_not(a_end)

    def a_goes_up(zp):
        return has_a(zp) & (zp <= z) & ((z < deep - 2) | ((z == deep - 2) & ((onward > 0) | (zp == 0))))

    def a_goes_down(zp):
        return has_a(zp) & (zp >= z) & ((z > 1) | ((z == 1) & ((onward < 0) | (zp == deep - 1))))

    def b_goes_up(zp):
        return has_b(zp) & (zp <= z) & ((z < deep - 2) | ((z == deep - 2) & ((onward < 0) | (zp == 0))))

    def b_goes_down(zp):
        return has_b(zp) & (zp >= z) & ((z > 1) | ((z == 1) & ((onward > 0) | (zp == deep - 1))))

    def crosses(zp):
        return (beyond(zp) & (through(zp) | jnp.logical_not(b_end))) | ((zp == z) & p_helper)

    def a_to_column(zp):
        relayed = q_helper & (zp == end)
        return (crosses(zp) & jnp.logical_not(relayed)) | ((zp == z) & a_end)

    def b_to_column(zp):
        return has_b(zp) & jnp.logical_not(helper & (zp == end))

    def has_b_far(zp):
        return through(zp) | jnp.logical_not(b_end)

    def has_f(zp):
        return (short(zp) & (through(zp) | jnp.logical_not(a_end))) | ((zp == z) & q_helper)

    def has_x(zp):
        return through(zp) | jnp.logical_not(a_end)

    size = rows // PARTS

    def transfer(send, source, target, zp, device, part):
        here = pl.ds(part * size, size)
        return pltpu.make_async_remote_copy(
            src_ref=held.at[slot(source, zp), here],
            dst_ref=held.at[slot(target, zp), here],
            send_sem=send_sem.at[send * deep + zp, part],
            recv_sem=recv_sem.at[slot(target, zp), part],
            device_id=device,
            device_id_type=MESH,
        )

    def arrived(kind, zp, part):
        transfer(A_UP, kind, kind, zp, sibling, part).wait_recv()

    def sent(send, zp):
        for part in range(PARTS):
            transfer(send, A_NEAR, A_NEAR, zp, sibling, part).wait_send()

    def unit(which):
        values = raw[which].astype(jnp.float32)
        inverse = lax.rsqrt(jnp.sum(values * values, axis=-1, keepdims=True) + 1e-06)
        return values * inverse, inverse

    barrier = pltpu.get_barrier_semaphore()
    for device in (sibling, after_same, before_same, before_other):
        pl.semaphore_signal(barrier, inc=1, device_id=device, device_id_type=MESH)

    @pl.when(z < deep - 1)
    def _():
        pl.semaphore_signal(barrier, inc=1, device_id=above, device_id_type=MESH)

    @pl.when(z > 0)
    def _():
        pl.semaphore_signal(barrier, inc=1, device_id=below, device_id_type=MESH)

    for copy in copies:
        copy.wait()
    held[slot(B_NEAR, z)] = unit(core)[0].astype(jnp.bfloat16)
    edges = jnp.where(z > 0, 1, 0) + jnp.where(z < deep - 1, 1, 0)
    pl.semaphore_wait(barrier, 4 + edges)

    def pass_b(zp, distance, part):
        @pl.when(has_b(zp) & (distance > 0))
        def _():
            arrived(B_NEAR, zp, part)

        @pl.when(b_goes_up(zp))
        def _():
            transfer(B_UP, B_NEAR, B_NEAR, zp, above, part).start()

        @pl.when(b_goes_down(zp))
        def _():
            transfer(B_DOWN, B_NEAR, B_NEAR, zp, below, part).start()

        @pl.when(b_to_column(zp))
        def _():
            transfer(B_COLUMN, B_NEAR, B_FAR, zp, before_other, part).start()

    def pass_a(zp, distance, part):
        @pl.when(has_a(zp) & (distance > 0))
        def _():
            arrived(A_NEAR, zp, part)

        @pl.when(a_goes_up(zp))
        def _():
            transfer(A_UP, A_NEAR, A_NEAR, zp, above, part).start()

        @pl.when(a_goes_down(zp))
        def _():
            transfer(A_DOWN, A_NEAR, A_NEAR, zp, below, part).start()

        @pl.when(a_to_column(zp))
        def _():
            transfer(A_COLUMN, A_NEAR, A_FAR, zp, after_same, part).start()

        @pl.when(has_a(zp))
        def _():
            transfer(A_CORE, A_NEAR, X_NEAR, zp, sibling, part).start()

    def relay():
        for part in range(PARTS):
            arrived(B_FAR, z, part)
            transfer(B_RELAY, B_FAR, B_FAR, z, inner, part).start()

            @pl.when(a_end)
            def _():
                arrived(A_FAR, z, part)
                transfer(A_RELAY, A_FAR, A_FAR, z, inner, part).start()

    def sum_copy():
        return pltpu.make_async_remote_copy(
            src_ref=sums.at[0],
            dst_ref=sums.at[1],
            send_sem=sum_sem.at[0],
            recv_sem=sum_sem.at[1],
            device_id=outer,
            device_id_type=MESH,
        )

    def loss_copy():
        return pltpu.make_async_remote_copy(
            src_ref=loss_row.at[0],
            dst_ref=loss_row.at[1],
            send_sem=sum_sem.at[2],
            recv_sem=sum_sem.at[3],
            device_id=outer,
            device_id_type=MESH,
        )

    diagonal = lax.broadcasted_iota(jnp.int32, (rows, rows), 0) == lax.broadcasted_iota(
        jnp.int32, (rows, rows), 1
    )

    def weigh(role, own, other, pairs, with_loss):
        dots = lax.dot_general(
            held[own],
            held[other],
            (((1,), (1,)), ((), ())),
            preferred_element_type=jnp.float32,
        )
        if not with_loss:
            power = jnp.exp2(dots * (-LOG2E * scale) - LOG2E * offset)
            return (scale / (1.0 + power)).astype(jnp.bfloat16)
        logits = scale * dots + offset
        turned = jnp.where(diagonal, -logits, logits) if pairs else logits
        small = jnp.exp(-jnp.abs(turned))
        loss = jnp.maximum(turned, 0.0) + jnp.log1p(small)
        part = loss[:, :LANES]
        for at in range(LANES, rows, LANES):
            part = part + loss[:, at : at + LANES]
        losses[role] += part
        weights = jnp.where(turned >= 0.0, scale, scale * small) / (1.0 + small)
        if pairs:
            weights = jnp.where(diagonal, -weights, weights)
        return weights.astype(jnp.bfloat16)

    def meet(role, own, other, pairs):
        def add(with_loss):
            weights = weigh(role, own, other, pairs, with_loss)
            step = 384 if width % 384 == 0 else width
            for at in range(0, width, step):
                total[role, :, at : at + step] += jnp.dot(
                    weights, held[other, :, at : at + step], preferred_element_type=jnp.float32
                )

        if pairs:
            add(True)
            return
        of_image = (role == core) | ((role == 2) & (z == 1))

        @pl.when(of_image)
        def _():
            add(True)

        @pl.when(jnp.logical_not(of_image))
        def _():
            add(False)

    own_a, own_b = slot(A_NEAR, z), slot(B_NEAR, z)

    def in_row(role):
        return lax.dot_general(
            jnp.ones((8, LANES), jnp.float32),
            losses[role],
            (((1,), (1,)), ((), ())),
            precision=lax.Precision.HIGHEST,
            preferred_element_type=jnp.float32,
        )

    def near(zp):
        first = jnp.where(short(zp), 0, jnp.where(beyond(zp), 1, 0))

        def tile(which, carry):
            @pl.when((which == 2) & has_x(zp))
            def _():
                for part in range(PARTS):
                    arrived(X_NEAR, zp, part)

            role = jnp.where(which == 0, 0, 1)
            kind = jnp.where(which == 0, A_NEAR, jnp.where(which == 1, B_NEAR, X_NEAR))
            own = jnp.where(which == 0, own_b, own_a)

            @pl.when((which < 2) & (zp == z))
            def _():
                meet(role, own, slot(kind, zp), True)

            @pl.when(((which == 2) & has_x(zp)) | ((which == first) & (zp != z)))
            def _():
                meet(role, own, slot(kind, zp), False)

            return carry

        lax.fori_loop(0, 3, tile, 0)

    def far(zp):
        @pl.when(has_b_far(zp))
        def _():
            for part in range(PARTS):

                @pl.when(jnp.logical_not(at_end & (zp == z)))
                def _():
                    arrived(B_FAR, zp, part)

                @pl.when(crosses(zp))
                def _():
                    transfer(F_CORE, B_FAR, F_FAR, zp, sibling, part).start()

        helps = helper & (zp != end) & (zp != last)

        def tile(which, carry):
            for part in range(PARTS):

                @pl.when((which == 1) & crosses(zp))
                def _():
                    arrived(A_FAR, zp, part)

                @pl.when((which == 1) & has_f(zp))
                def _():
                    arrived(F_FAR, zp, part)

            helping = which < 2
            kind_0 = jnp.where(q_helper, X_NEAR, B_FAR)
            kind_1 = jnp.where(q_helper, F_FAR, A_FAR)
            kind_3 = jnp.where(short(zp), F_FAR, A_FAR)
            kind = jnp.where(
                which == 0,
                kind_0,
                jnp.where(which == 1, kind_1, jnp.where(which == 2, B_FAR, kind_3)),
            )
            in_q = (which == 3) & short(zp)
            own_end = jnp.where(q_helper, slot(A_NEAR, end), slot(B_NEAR, end))
            own = jnp.where(helping, own_end, jnp.where(in_q, own_a, own_b))
            role = jnp.where(helping, 2, jnp.where(in_q, 1, 0))
            other = (zp != z) & (through(zp) | jnp.logical_not(at_end))

            @pl.when(
                (helping & helps)
                | ((which == 2) & has_b_far(zp))
                | ((which == 3) & other)
            )
            def _():
                meet(role, own, slot(kind, zp), False)

            @pl.when((which == 1) & helper & (zp == final))
            def _():
                sums[0] = total[2].astype(jnp.bfloat16)
                sum_copy().start()

                @pl.when(z == 1)
                def _():
                    loss_row[0] = in_row(2)
                    loss_copy().start()

            return carry

        lax.fori_loop(0, 4, tile, 0)

    inward = jnp.where(z < deep // 2, 1, -1)

    def both_ways(distance, action):
        ahead, behind = z + inward * distance, z - inward * distance

        @pl.when((distance >= 0) & (distance < deep) & (ahead >= 0) & (ahead < deep))
        def _():
            action(ahead)

        @pl.when((distance > 0) & (behind >= 0) & (behind < deep))
        def _():
            action(behind)

    def turn(distance, carry):
        for part in range(PARTS):
            both_ways(distance, functools.partial(pass_b, distance=distance, part=part))

        @pl.when(distance == 0)
        def _():
            held[slot(A_NEAR, z)] = unit(1 - core)[0].astype(jnp.bfloat16)

        for part in range(PARTS):
            both_ways(distance, functools.partial(pass_a, distance=distance, part=part))

        @pl.when(distance == 0)
        def _():
            total[...] = jnp.zeros_like(total)
            losses[...] = jnp.zeros_like(losses)

        both_ways(distance, near)
        pl.when((distance == 0) & at_end)(relay)
        both_ways(distance - 1, far)
        return carry

    lax.fori_loop(0, deep + 1, turn, 0)

    @pl.when(at_end)
    def _():
        sum_copy().wait_recv()
        role = jnp.where(a_end, 1, 0)
        total[role] += sums[1].astype(jnp.float32)

    def finish(which, role):
        unit32, inverse = unit(which)
        grad = total[role]
        along = jnp.sum(unit32 * grad, axis=-1, keepdims=True)
        return inverse * (grad - unit32 * along)

    grad_img_ref[...] = finish(0, core)
    grad_txt_ref[...] = finish(1, 1 - core)
    loss_ref[...] = in_row(core)[0:1]

    @pl.when(z == 0)
    def _():
        loss_copy().wait_recv()
        loss_ref[...] += loss_row[1, 0:1]

    def settle(zp, carry):
        for went, send in (
            (a_goes_up(zp), A_UP),
            (a_goes_down(zp), A_DOWN),
            (b_goes_up(zp), B_UP),
            (b_goes_down(zp), B_DOWN),
            (has_a(zp), A_CORE),
            (a_to_column(zp), A_COLUMN),
            (b_to_column(zp), B_COLUMN),
            (crosses(zp), F_CORE),
            ((zp == z) & a_end, A_RELAY),
            ((zp == z) & at_end, B_RELAY),
        ):
            pl.when(went)(functools.partial(sent, send, zp))
        return carry

    lax.fori_loop(0, deep, settle, 0)

    @pl.when(helper)
    def _():
        sum_copy().wait_send()
        pl.when(z == 1)(lambda: loss_copy().wait_send())


def on_column(columns, deep, images, texts, scale, offset):
    rows, width = images.shape
    tiles = 4 * deep
    loss, grad_images, grad_texts = pl.pallas_call(
        functools.partial(column_kernel, columns, deep),
        out_shape=(
            jax.ShapeDtypeStruct((1, rows), jnp.float32),
            jax.ShapeDtypeStruct((rows, width), jnp.float32),
            jax.ShapeDtypeStruct((rows, width), jnp.float32),
        ),
        in_specs=[pl.BlockSpec(memory_space=pltpu.SMEM)] * 2
        + [pl.BlockSpec(memory_space=pl.ANY)] * 2,
        out_specs=[pl.BlockSpec(memory_space=pltpu.VMEM)] * 3,
        scratch_shapes=[
            pltpu.VMEM((KINDS * deep, rows, width), jnp.bfloat16),
            pltpu.VMEM((3, rows, width), jnp.float32),
            pltpu.VMEM((3, rows, LANES), jnp.float32),
            pltpu.VMEM((2, rows, width), jnp.bfloat16),
            pltpu.VMEM((2, 8, rows), jnp.float32),
            pltpu.VMEM((2, rows, width), jnp.bfloat16),
            pltpu.SemaphoreType.DMA((2,)),
            pltpu.SemaphoreType.DMA((SENDS * deep, PARTS)),
            pltpu.SemaphoreType.DMA((KINDS * deep, PARTS)),
            pltpu.SemaphoreType.DMA((4,)),
        ],
        compiler_params=pltpu.CompilerParams(
            collective_id=0, has_side_effects=True, vmem_limit_bytes=48 * 1024 * 1024
        ),
        cost_estimate=pl.CostEstimate(
            flops=tiles * 4 * rows * rows * width,
            bytes_accessed=12 * rows * width,
            transcendentals=tiles * 3 * rows * rows,
        ),
        name="column",
    )(scale, offset, images, texts)
    return loss.reshape(rows), grad_images, grad_texts


def solution(mesh):
    blocks, deep = mesh.shape["blk"], mesh.shape["grp"]
    body = on_device
    if KSTEPS == 2 * deep and deep >= 4 and blocks % 2 == 0 and blocks >= 6:
        body = functools.partial(on_column, blocks // 2, deep)
    return jax.shard_map(
        body,
        mesh=mesh,
        in_specs=(P(("blk", "grp"), None), P(("blk", "grp"), None), P(), P()),
        out_specs=(P(("blk", "grp")), P(("blk", "grp"), None), P(("blk", "grp"), None)),
        check_vma=False,
    )
```

```python
import functools

import jax
import jax.numpy as jnp
from jax import lax
from jax.experimental import pallas as pl
from jax.experimental.pallas import tpu as pltpu
from jax.sharding import PartitionSpec as P

KSTEPS = 8


def passed_along(block, axis, distance):
    devices = range(lax.axis_size(axis))
    route = [((i - distance) % len(devices), i) for i in devices]
    return lax.ppermute(block, axis, route)


def normalize(raw):
    computed_quantities = raw.astype(jnp.float32)
    inverse = lax.rsqrt(
        jnp.sum(computed_quantities * computed_quantities, axis=-1, keepdims=True) + 1e-06
    )
    return (computed_quantities * inverse, inverse)


def back_norm(unit32, inverse, grad_unit):
    along = jnp.sum(unit32 * grad_unit, axis=-1, keepdims=True)
    return inverse * (grad_unit - unit32 * along)


def pairwise_loss_terms(
    image_block_rows, text_block_rows, target_labels, smoothing_coefficient, block_displacement
):
    pair_logit_matrix = (
        smoothing_coefficient
        * lax.dot_general(
            image_block_rows,
            text_block_rows,
            (((1,), (1,)), ((), ())),
            preferred_element_type=jnp.float32,
        )
        + block_displacement
    )
    row_portion = jnp.sum(jax.nn.softplus(-target_labels * pair_logit_matrix), axis=-1)
    sigmoid_weights = (
        -target_labels * jax.nn.sigmoid(-target_labels * pair_logit_matrix) * smoothing_coefficient
    ).astype(jnp.bfloat16)
    return (row_portion, sigmoid_weights)


def image_side(sigmoid_weights, text_block_rows):
    return jnp.dot(sigmoid_weights, text_block_rows, preferred_element_type=jnp.float32)


def text_side(sigmoid_weights, image_block_rows):
    return lax.dot_general(
        sigmoid_weights,
        image_block_rows,
        (((0,), (0,)), ((), ())),
        preferred_element_type=jnp.float32,
    )


def on_device(picture_embedding_array, caption_embedding_array, sharpness_multiplier, score_offset):
    smoothing_coefficient = sharpness_multiplier[0]
    block_displacement = score_offset[0]
    rows = picture_embedding_array.shape[0]
    img_unit32, img_inverse = normalize(picture_embedding_array)
    txt_unit32, txt_inverse = normalize(caption_embedding_array)
    image_unit_vectors = img_unit32.astype(jnp.bfloat16)
    text_unit_vectors = txt_unit32.astype(jnp.bfloat16)
    positions = lax.broadcasted_iota(jnp.int32, (rows, rows), 0)
    columns = lax.broadcasted_iota(jnp.int32, (rows, rows), 1)
    initial_label_values = jnp.where(positions == columns, 1.0, -1.0).astype(jnp.float32)
    negative_labels = jnp.full((rows, rows), -1.0, jnp.float32)
    row_total_sum, sigmoid_weights = pairwise_loss_terms(
        image_unit_vectors,
        text_unit_vectors,
        initial_label_values,
        smoothing_coefficient,
        block_displacement,
    )
    grad_img = image_side(sigmoid_weights, text_unit_vectors)
    own_text = text_side(sigmoid_weights, image_unit_vectors)
    incoming_caption_groups = text_unit_vectors
    carried = own_text
    for hop_index in range(1, KSTEPS):
        incoming_caption_groups, carried = (
            passed_along(incoming_caption_groups, ("blk", "grp"), 1),
            passed_along(carried.astype(jnp.bfloat16), ("blk", "grp"), 1).astype(carried.dtype),
        )
        row_portion, sigmoid_weights = pairwise_loss_terms(
            image_unit_vectors,
            incoming_caption_groups,
            negative_labels,
            smoothing_coefficient,
            block_displacement,
        )
        row_total_sum = row_total_sum + row_portion
        grad_img = grad_img + image_side(sigmoid_weights, incoming_caption_groups)
        carried = carried + text_side(sigmoid_weights, image_unit_vectors)
    grad_txt = passed_along(carried.astype(jnp.bfloat16), ("blk", "grp"), 1 - KSTEPS).astype(
        carried.dtype
    )
    grad_images = back_norm(img_unit32, img_inverse, grad_img)
    grad_texts = back_norm(txt_unit32, txt_inverse, grad_txt)
    return (row_total_sum, grad_images, grad_texts)


MESH = pl.DeviceIdType.MESH
A_NEAR, B_NEAR, X_NEAR, A_FAR, B_FAR, F_FAR = range(6)
KINDS = 6
A_UP, A_DOWN, B_UP, B_DOWN, A_CORE, A_COLUMN, B_COLUMN, F_CORE, A_RELAY, B_RELAY = range(10)
SENDS = 10
LANES = 128
LOG2E = 1.4426950408889634
PARTS = 4


def column_kernel(
    columns,
    deep,
    scale_ref,
    offset_ref,
    img_hbm,
    txt_hbm,
    loss_ref,
    grad_img_ref,
    grad_txt_ref,
    held,
    total,
    losses,
    sums,
    loss_row,
    raw,
    raw_sem,
    send_sem,
    recv_sem,
    sum_sem,
):
    blk = lax.axis_index("blk")
    z = lax.axis_index("grp")
    core = lax.rem(blk, 2)
    column = blk // 2
    onward = 1 - 2 * core
    after = lax.rem(column + onward + columns, columns)
    before = lax.rem(column - onward + columns, columns)
    sibling = (2 * column + 1 - core, z)
    above, below = (blk, z + 1), (blk, z - 1)
    after_same = (2 * after + core, z)
    before_same = (2 * before + core, z)
    before_other = (2 * before + 1 - core, z)
    rows, width = img_hbm.shape
    copies = [
        pltpu.make_async_copy(source, raw.at[at], raw_sem.at[at])
        for at, source in enumerate((img_hbm, txt_hbm))
    ]
    for copy in copies:
        copy.start()
    scale, offset = scale_ref[0], offset_ref[0]

    def beyond(zp):
        return (zp - z) * onward > 0

    def short(zp):
        return (zp - z) * onward < 0

    def slot(kind, zp):
        return kind * deep + zp

    at_end = (z == 0) | (z == deep - 1)
    a_end = jnp.where(onward > 0, z == deep - 1, z == 0)
    b_end = jnp.where(onward > 0, z == 0, z == deep - 1)
    q_helper = jnp.where(onward > 0, z == deep - 2, z == 1)
    p_helper = jnp.where(onward > 0, z == 1, z == deep - 2)
    helper = (z == 1) | (z == deep - 2)
    end = jnp.where(z == 1, 0, deep - 1)
    last = deep - 1 - end
    inner = (blk, jnp.where(z == 0, 1, deep - 2))
    outer = (blk, end)

    final = jnp.where(end == 0, deep - 2, 1)

    def through(zp):
        return (zp == z) | (zp == deep - 1 - z)

    def has_a(zp):
        return through(zp) | jnp.logical_not(b_end)

    def has_b(zp):
        return through(zp) | jnp.logical_not(a_end)

    def a_goes_up(zp):
        return has_a(zp) & (zp <= z) & ((z < deep - 2) | ((z == deep - 2) & ((onward > 0) | (zp == 0))))

    def a_goes_down(zp):
        return has_a(zp) & (zp >= z) & ((z > 1) | ((z == 1) & ((onward < 0) | (zp == deep - 1))))

    def b_goes_up(zp):
        return has_b(zp) & (zp <= z) & ((z < deep - 2) | ((z == deep - 2) & ((onward < 0) | (zp == 0))))

    def b_goes_down(zp):
        return has_b(zp) & (zp >= z) & ((z > 1) | ((z == 1) & ((onward > 0) | (zp == deep - 1))))

    def crosses(zp):
        return (beyond(zp) & (through(zp) | jnp.logical_not(b_end))) | ((zp == z) & p_helper)

    def a_to_column(zp):
        relayed = q_helper & (zp == end)
        return (crosses(zp) & jnp.logical_not(relayed)) | ((zp == z) & a_end)

    def b_to_column(zp):
        return has_b(zp) & jnp.logical_not(helper & (zp == end))

    def has_b_far(zp):
        return through(zp) | jnp.logical_not(b_end)

    def has_f(zp):
        return (short(zp) & (through(zp) | jnp.logical_not(a_end))) | ((zp == z) & q_helper)

    def has_x(zp):
        return through(zp) | jnp.logical_not(a_end)

    size = rows // PARTS

    def transfer(send, source, target, zp, device, part):
        here = pl.ds(part * size, size)
        return pltpu.make_async_remote_copy(
            src_ref=held.at[slot(source, zp), here],
            dst_ref=held.at[slot(target, zp), here],
            send_sem=send_sem.at[send * deep + zp, part],
            recv_sem=recv_sem.at[slot(target, zp), part],
            device_id=device,
            device_id_type=MESH,
        )

    def arrived(kind, zp, part):
        transfer(A_UP, kind, kind, zp, sibling, part).wait_recv()

    def sent(send, zp):
        for part in range(PARTS):
            transfer(send, A_NEAR, A_NEAR, zp, sibling, part).wait_send()

    def unit(which):
        values = raw[which].astype(jnp.float32)
        inverse = lax.rsqrt(jnp.sum(values * values, axis=-1, keepdims=True) + 1e-06)
        return values * inverse, inverse

    barrier = pltpu.get_barrier_semaphore()
    for device in (sibling, after_same, before_same, before_other):
        pl.semaphore_signal(barrier, inc=1, device_id=device, device_id_type=MESH)

    @pl.when(z < deep - 1)
    def _():
        pl.semaphore_signal(barrier, inc=1, device_id=above, device_id_type=MESH)

    @pl.when(z > 0)
    def _():
        pl.semaphore_signal(barrier, inc=1, device_id=below, device_id_type=MESH)

    for copy in copies:
        copy.wait()
    held[slot(B_NEAR, z)] = unit(core)[0].astype(jnp.bfloat16)
    edges = jnp.where(z > 0, 1, 0) + jnp.where(z < deep - 1, 1, 0)
    pl.semaphore_wait(barrier, 4 + edges)

    def pass_b(zp, distance, part):
        @pl.when(has_b(zp) & (distance > 0))
        def _():
            arrived(B_NEAR, zp, part)

        @pl.when(b_goes_up(zp))
        def _():
            transfer(B_UP, B_NEAR, B_NEAR, zp, above, part).start()

        @pl.when(b_goes_down(zp))
        def _():
            transfer(B_DOWN, B_NEAR, B_NEAR, zp, below, part).start()

        @pl.when(b_to_column(zp))
        def _():
            transfer(B_COLUMN, B_NEAR, B_FAR, zp, before_other, part).start()

    def pass_a(zp, distance, part):
        @pl.when(has_a(zp) & (distance > 0))
        def _():
            arrived(A_NEAR, zp, part)

        @pl.when(a_goes_up(zp))
        def _():
            transfer(A_UP, A_NEAR, A_NEAR, zp, above, part).start()

        @pl.when(a_goes_down(zp))
        def _():
            transfer(A_DOWN, A_NEAR, A_NEAR, zp, below, part).start()

        @pl.when(a_to_column(zp))
        def _():
            transfer(A_COLUMN, A_NEAR, A_FAR, zp, after_same, part).start()

        @pl.when(has_a(zp))
        def _():
            transfer(A_CORE, A_NEAR, X_NEAR, zp, sibling, part).start()

    def relay():
        for part in range(PARTS):
            arrived(B_FAR, z, part)
            transfer(B_RELAY, B_FAR, B_FAR, z, inner, part).start()

            @pl.when(a_end)
            def _():
                arrived(A_FAR, z, part)
                transfer(A_RELAY, A_FAR, A_FAR, z, inner, part).start()

    def sum_copy():
        return pltpu.make_async_remote_copy(
            src_ref=sums.at[0],
            dst_ref=sums.at[1],
            send_sem=sum_sem.at[0],
            recv_sem=sum_sem.at[1],
            device_id=outer,
            device_id_type=MESH,
        )

    def loss_copy():
        return pltpu.make_async_remote_copy(
            src_ref=loss_row.at[0],
            dst_ref=loss_row.at[1],
            send_sem=sum_sem.at[2],
            recv_sem=sum_sem.at[3],
            device_id=outer,
            device_id_type=MESH,
        )

    diagonal = lax.broadcasted_iota(jnp.int32, (rows, rows), 0) == lax.broadcasted_iota(
        jnp.int32, (rows, rows), 1
    )

    def weigh(role, own, other, pairs, with_loss):
        dots = lax.dot_general(
            held[own],
            held[other],
            (((1,), (1,)), ((), ())),
            preferred_element_type=jnp.float32,
        )
        if not with_loss:
            power = jnp.exp2(dots * (-LOG2E * scale) - LOG2E * offset)
            return (scale / (1.0 + power)).astype(jnp.bfloat16)
        logits = scale * dots + offset
        turned = jnp.where(diagonal, -logits, logits) if pairs else logits
        small = jnp.exp(-jnp.abs(turned))
        loss = jnp.maximum(turned, 0.0) + jnp.log1p(small)
        part = loss[:, :LANES]
        for at in range(LANES, rows, LANES):
            part = part + loss[:, at : at + LANES]
        losses[role] += part
        weights = jnp.where(turned >= 0.0, scale, scale * small) / (1.0 + small)
        if pairs:
            weights = jnp.where(diagonal, -weights, weights)
        return weights.astype(jnp.bfloat16)

    def meet(role, own, other, pairs):
        def add(with_loss):
            weights = weigh(role, own, other, pairs, with_loss)
            step = 384 if width % 384 == 0 else width
            for at in range(0, width, step):
                total[role, :, at : at + step] += jnp.dot(
                    weights, held[other, :, at : at + step], preferred_element_type=jnp.float32
                )

        if pairs:
            add(True)
            return
        of_image = (role == core) | ((role == 2) & (z == 1))

        @pl.when(of_image)
        def _():
            add(True)

        @pl.when(jnp.logical_not(of_image))
        def _():
            add(False)

    own_a, own_b = slot(A_NEAR, z), slot(B_NEAR, z)

    def in_row(role):
        return lax.dot_general(
            jnp.ones((8, LANES), jnp.float32),
            losses[role],
            (((1,), (1,)), ((), ())),
            precision=lax.Precision.HIGHEST,
            preferred_element_type=jnp.float32,
        )

    def near(zp):
        first = jnp.where(short(zp), 0, jnp.where(beyond(zp), 1, 0))

        def tile(which, carry):
            @pl.when((which == 2) & has_x(zp))
            def _():
                for part in range(PARTS):
                    arrived(X_NEAR, zp, part)

            role = jnp.where(which == 0, 0, 1)
            kind = jnp.where(which == 0, A_NEAR, jnp.where(which == 1, B_NEAR, X_NEAR))
            own = jnp.where(which == 0, own_b, own_a)

            @pl.when((which < 2) & (zp == z))
            def _():
                meet(role, own, slot(kind, zp), True)

            @pl.when(((which == 2) & has_x(zp)) | ((which == first) & (zp != z)))
            def _():
                meet(role, own, slot(kind, zp), False)

            return carry

        lax.fori_loop(0, 3, tile, 0)

    def far(zp):
        @pl.when(has_b_far(zp))
        def _():
            for part in range(PARTS):

                @pl.when(jnp.logical_not(at_end & (zp == z)))
                def _():
                    arrived(B_FAR, zp, part)

                @pl.when(crosses(zp))
                def _():
                    transfer(F_CORE, B_FAR, F_FAR, zp, sibling, part).start()

        helps = helper & (zp != end) & (zp != last)

        def tile(which, carry):
            for part in range(PARTS):

                @pl.when((which == 1) & crosses(zp))
                def _():
                    arrived(A_FAR, zp, part)

                @pl.when((which == 1) & has_f(zp))
                def _():
                    arrived(F_FAR, zp, part)

            helping = which < 2
            kind_0 = jnp.where(q_helper, X_NEAR, B_FAR)
            kind_1 = jnp.where(q_helper, F_FAR, A_FAR)
            kind_3 = jnp.where(short(zp), F_FAR, A_FAR)
            kind = jnp.where(
                which == 0,
                kind_0,
                jnp.where(which == 1, kind_1, jnp.where(which == 2, B_FAR, kind_3)),
            )
            in_q = (which == 3) & short(zp)
            own_end = jnp.where(q_helper, slot(A_NEAR, end), slot(B_NEAR, end))
            own = jnp.where(helping, own_end, jnp.where(in_q, own_a, own_b))
            role = jnp.where(helping, 2, jnp.where(in_q, 1, 0))
            other = (zp != z) & (through(zp) | jnp.logical_not(at_end))

            @pl.when(
                (helping & helps)
                | ((which == 2) & has_b_far(zp))
                | ((which == 3) & other)
            )
            def _():
                meet(role, own, slot(kind, zp), False)

            @pl.when((which == 1) & helper & (zp == final))
            def _():
                sums[0] = total[2].astype(jnp.bfloat16)
                sum_copy().start()

                @pl.when(z == 1)
                def _():
                    loss_row[0] = in_row(2)
                    loss_copy().start()

            return carry

        lax.fori_loop(0, 4, tile, 0)

    inward = jnp.where(z < deep // 2, 1, -1)

    def both_ways(distance, action):
        ahead, behind = z + inward * distance, z - inward * distance

        @pl.when((distance >= 0) & (distance < deep) & (ahead >= 0) & (ahead < deep))
        def _():
            action(ahead)

        @pl.when((distance > 0) & (behind >= 0) & (behind < deep))
        def _():
            action(behind)

    def turn(distance, carry):
        for part in range(PARTS):
            both_ways(distance, functools.partial(pass_b, distance=distance, part=part))

        @pl.when(distance == 0)
        def _():
            held[slot(A_NEAR, z)] = unit(1 - core)[0].astype(jnp.bfloat16)

        for part in range(PARTS):
            both_ways(distance, functools.partial(pass_a, distance=distance, part=part))

        @pl.when(distance == 0)
        def _():
            total[...] = jnp.zeros_like(total)
            losses[...] = jnp.zeros_like(losses)

        both_ways(distance, near)
        pl.when((distance == 0) & at_end)(relay)
        both_ways(distance - 1, far)
        return carry

    lax.fori_loop(0, deep + 1, turn, 0)

    def finish(which, role, ref):
        unit32, inverse = unit(which)
        grad = total[role]
        along = jnp.sum(unit32 * grad, axis=-1, keepdims=True)
        ref[...] = inverse * (grad - unit32 * along)

    def finish_images():
        finish(0, core, grad_img_ref)

    def finish_texts():
        finish(1, 1 - core, grad_txt_ref)

    pl.when(z == 0)(finish_texts)
    pl.when(z != 0)(finish_images)

    @pl.when(at_end)
    def _():
        sum_copy().wait_recv()
        role = jnp.where(a_end, 1, 0)
        total[role] += sums[1].astype(jnp.float32)

    pl.when(z == 0)(finish_images)
    pl.when(z != 0)(finish_texts)
    loss_ref[...] = in_row(core)[0:1]

    @pl.when(z == 0)
    def _():
        loss_copy().wait_recv()
        loss_ref[...] += loss_row[1, 0:1]

    def settle(zp, carry):
        for went, send in (
            (a_goes_up(zp), A_UP),
            (a_goes_down(zp), A_DOWN),
            (b_goes_up(zp), B_UP),
            (b_goes_down(zp), B_DOWN),
            (has_a(zp), A_CORE),
            (a_to_column(zp), A_COLUMN),
            (b_to_column(zp), B_COLUMN),
            (crosses(zp), F_CORE),
            ((zp == z) & a_end, A_RELAY),
            ((zp == z) & at_end, B_RELAY),
        ):
            pl.when(went)(functools.partial(sent, send, zp))
        return carry

    lax.fori_loop(0, deep, settle, 0)

    @pl.when(helper)
    def _():
        sum_copy().wait_send()
        pl.when(z == 1)(lambda: loss_copy().wait_send())


def on_column(columns, deep, images, texts, scale, offset):
    rows, width = images.shape
    tiles = 4 * deep
    loss, grad_images, grad_texts = pl.pallas_call(
        functools.partial(column_kernel, columns, deep),
        out_shape=(
            jax.ShapeDtypeStruct((1, rows), jnp.float32),
            jax.ShapeDtypeStruct((rows, width), jnp.float32),
            jax.ShapeDtypeStruct((rows, width), jnp.float32),
        ),
        in_specs=[pl.BlockSpec(memory_space=pltpu.SMEM)] * 2
        + [pl.BlockSpec(memory_space=pl.ANY)] * 2,
        out_specs=[pl.BlockSpec(memory_space=pltpu.VMEM)] * 3,
        scratch_shapes=[
            pltpu.VMEM((KINDS * deep, rows, width), jnp.bfloat16),
            pltpu.VMEM((3, rows, width), jnp.float32),
            pltpu.VMEM((3, rows, LANES), jnp.float32),
            pltpu.VMEM((2, rows, width), jnp.bfloat16),
            pltpu.VMEM((2, 8, rows), jnp.float32),
            pltpu.VMEM((2, rows, width), jnp.bfloat16),
            pltpu.SemaphoreType.DMA((2,)),
            pltpu.SemaphoreType.DMA((SENDS * deep, PARTS)),
            pltpu.SemaphoreType.DMA((KINDS * deep, PARTS)),
            pltpu.SemaphoreType.DMA((4,)),
        ],
        compiler_params=pltpu.CompilerParams(
            collective_id=0, has_side_effects=True, vmem_limit_bytes=48 * 1024 * 1024
        ),
        cost_estimate=pl.CostEstimate(
            flops=tiles * 4 * rows * rows * width,
            bytes_accessed=12 * rows * width,
            transcendentals=tiles * 3 * rows * rows,
        ),
        name="column",
    )(scale, offset, images, texts)
    return loss.reshape(rows), grad_images, grad_texts


def solution(mesh):
    blocks, deep = mesh.shape["blk"], mesh.shape["grp"]
    body = on_device
    if KSTEPS == 2 * deep and deep >= 4 and blocks % 2 == 0 and blocks >= 6:
        body = functools.partial(on_column, blocks // 2, deep)
    return jax.shard_map(
        body,
        mesh=mesh,
        in_specs=(P(("blk", "grp"), None), P(("blk", "grp"), None), P(), P()),
        out_specs=(P(("blk", "grp")), P(("blk", "grp"), None), P(("blk", "grp"), None)),
        check_vma=False,
    )
```

```python
import functools

import jax
import jax.numpy as jnp
from jax import lax
from jax.experimental import pallas as pl
from jax.experimental.pallas import tpu as pltpu
from jax.sharding import PartitionSpec as P

KSTEPS = 8


def passed_along(block, axis, distance):
    devices = range(lax.axis_size(axis))
    route = [((i - distance) % len(devices), i) for i in devices]
    return lax.ppermute(block, axis, route)


def normalize(raw):
    computed_quantities = raw.astype(jnp.float32)
    inverse = lax.rsqrt(
        jnp.sum(computed_quantities * computed_quantities, axis=-1, keepdims=True) + 1e-06
    )
    return (computed_quantities * inverse, inverse)


def back_norm(unit32, inverse, grad_unit):
    along = jnp.sum(unit32 * grad_unit, axis=-1, keepdims=True)
    return inverse * (grad_unit - unit32 * along)


def pairwise_loss_terms(
    image_block_rows, text_block_rows, target_labels, smoothing_coefficient, block_displacement
):
    pair_logit_matrix = (
        smoothing_coefficient
        * lax.dot_general(
            image_block_rows,
            text_block_rows,
            (((1,), (1,)), ((), ())),
            preferred_element_type=jnp.float32,
        )
        + block_displacement
    )
    row_portion = jnp.sum(jax.nn.softplus(-target_labels * pair_logit_matrix), axis=-1)
    sigmoid_weights = (
        -target_labels * jax.nn.sigmoid(-target_labels * pair_logit_matrix) * smoothing_coefficient
    ).astype(jnp.bfloat16)
    return (row_portion, sigmoid_weights)


def image_side(sigmoid_weights, text_block_rows):
    return jnp.dot(sigmoid_weights, text_block_rows, preferred_element_type=jnp.float32)


def text_side(sigmoid_weights, image_block_rows):
    return lax.dot_general(
        sigmoid_weights,
        image_block_rows,
        (((0,), (0,)), ((), ())),
        preferred_element_type=jnp.float32,
    )


def on_device(picture_embedding_array, caption_embedding_array, sharpness_multiplier, score_offset):
    smoothing_coefficient = sharpness_multiplier[0]
    block_displacement = score_offset[0]
    rows = picture_embedding_array.shape[0]
    img_unit32, img_inverse = normalize(picture_embedding_array)
    txt_unit32, txt_inverse = normalize(caption_embedding_array)
    image_unit_vectors = img_unit32.astype(jnp.bfloat16)
    text_unit_vectors = txt_unit32.astype(jnp.bfloat16)
    positions = lax.broadcasted_iota(jnp.int32, (rows, rows), 0)
    columns = lax.broadcasted_iota(jnp.int32, (rows, rows), 1)
    initial_label_values = jnp.where(positions == columns, 1.0, -1.0).astype(jnp.float32)
    negative_labels = jnp.full((rows, rows), -1.0, jnp.float32)
    row_total_sum, sigmoid_weights = pairwise_loss_terms(
        image_unit_vectors,
        text_unit_vectors,
        initial_label_values,
        smoothing_coefficient,
        block_displacement,
    )
    grad_img = image_side(sigmoid_weights, text_unit_vectors)
    own_text = text_side(sigmoid_weights, image_unit_vectors)
    incoming_caption_groups = text_unit_vectors
    carried = own_text
    for hop_index in range(1, KSTEPS):
        incoming_caption_groups, carried = (
            passed_along(incoming_caption_groups, ("blk", "grp"), 1),
            passed_along(carried.astype(jnp.bfloat16), ("blk", "grp"), 1).astype(carried.dtype),
        )
        row_portion, sigmoid_weights = pairwise_loss_terms(
            image_unit_vectors,
            incoming_caption_groups,
            negative_labels,
            smoothing_coefficient,
            block_displacement,
        )
        row_total_sum = row_total_sum + row_portion
        grad_img = grad_img + image_side(sigmoid_weights, incoming_caption_groups)
        carried = carried + text_side(sigmoid_weights, image_unit_vectors)
    grad_txt = passed_along(carried.astype(jnp.bfloat16), ("blk", "grp"), 1 - KSTEPS).astype(
        carried.dtype
    )
    grad_images = back_norm(img_unit32, img_inverse, grad_img)
    grad_texts = back_norm(txt_unit32, txt_inverse, grad_txt)
    return (row_total_sum, grad_images, grad_texts)


MESH = pl.DeviceIdType.MESH
A_NEAR, B_NEAR, X_NEAR, A_FAR, B_FAR, F_FAR = range(6)
KINDS = 6
A_UP, A_DOWN, B_UP, B_DOWN, A_CORE, A_COLUMN, B_COLUMN, F_CORE, A_RELAY, B_RELAY = range(10)
SENDS = 10
LANES = 128
LOG2E = 1.4426950408889634
PARTS = 2


def column_kernel(
    columns,
    deep,
    scale_ref,
    offset_ref,
    img_hbm,
    txt_hbm,
    loss_ref,
    grad_img_ref,
    grad_txt_ref,
    held,
    total,
    losses,
    sums,
    loss_row,
    raw,
    raw_sem,
    send_sem,
    recv_sem,
    sum_sem,
):
    blk = lax.axis_index("blk")
    z = lax.axis_index("grp")
    core = lax.rem(blk, 2)
    column = blk // 2
    onward = 1 - 2 * core
    after = lax.rem(column + onward + columns, columns)
    before = lax.rem(column - onward + columns, columns)
    sibling = (2 * column + 1 - core, z)
    above, below = (blk, z + 1), (blk, z - 1)
    after_same = (2 * after + core, z)
    before_same = (2 * before + core, z)
    before_other = (2 * before + 1 - core, z)
    rows, width = img_hbm.shape
    copies = [
        pltpu.make_async_copy(source, raw.at[at], raw_sem.at[at])
        for at, source in enumerate((img_hbm, txt_hbm))
    ]
    for copy in copies:
        copy.start()
    scale, offset = scale_ref[0], offset_ref[0]

    def beyond(zp):
        return (zp - z) * onward > 0

    def short(zp):
        return (zp - z) * onward < 0

    def slot(kind, zp):
        return kind * deep + zp

    at_end = (z == 0) | (z == deep - 1)
    a_end = jnp.where(onward > 0, z == deep - 1, z == 0)
    b_end = jnp.where(onward > 0, z == 0, z == deep - 1)
    q_helper = jnp.where(onward > 0, z == deep - 2, z == 1)
    p_helper = jnp.where(onward > 0, z == 1, z == deep - 2)
    helper = (z == 1) | (z == deep - 2)
    end = jnp.where(z == 1, 0, deep - 1)
    last = deep - 1 - end
    inner = (blk, jnp.where(z == 0, 1, deep - 2))
    outer = (blk, end)

    final = jnp.where(end == 0, deep - 2, 1)

    def through(zp):
        return (zp == z) | (zp == deep - 1 - z)

    def has_a(zp):
        return through(zp) | jnp.logical_not(b_end)

    def has_b(zp):
        return through(zp) | jnp.logical_not(a_end)

    def a_goes_up(zp):
        return has_a(zp) & (zp <= z) & ((z < deep - 2) | ((z == deep - 2) & ((onward > 0) | (zp == 0))))

    def a_goes_down(zp):
        return has_a(zp) & (zp >= z) & ((z > 1) | ((z == 1) & ((onward < 0) | (zp == deep - 1))))

    def b_goes_up(zp):
        return has_b(zp) & (zp <= z) & ((z < deep - 2) | ((z == deep - 2) & ((onward < 0) | (zp == 0))))

    def b_goes_down(zp):
        return has_b(zp) & (zp >= z) & ((z > 1) | ((z == 1) & ((onward > 0) | (zp == deep - 1))))

    def crosses(zp):
        return (beyond(zp) & (through(zp) | jnp.logical_not(b_end))) | ((zp == z) & p_helper)

    def a_to_column(zp):
        relayed = q_helper & (zp == end)
        return (crosses(zp) & jnp.logical_not(relayed)) | ((zp == z) & a_end)

    def b_to_column(zp):
        return has_b(zp) & jnp.logical_not(helper & (zp == end))

    def has_b_far(zp):
        return through(zp) | jnp.logical_not(b_end)

    def has_f(zp):
        return (short(zp) & (through(zp) | jnp.logical_not(a_end))) | ((zp == z) & q_helper)

    def has_x(zp):
        return through(zp) | jnp.logical_not(a_end)

    size = rows // PARTS

    def transfer(send, source, target, zp, device, part):
        here = pl.ds(part * size, size)
        return pltpu.make_async_remote_copy(
            src_ref=held.at[slot(source, zp), here],
            dst_ref=held.at[slot(target, zp), here],
            send_sem=send_sem.at[send * deep + zp, part],
            recv_sem=recv_sem.at[slot(target, zp), part],
            device_id=device,
            device_id_type=MESH,
        )

    def arrived(kind, zp, part):
        transfer(A_UP, kind, kind, zp, sibling, part).wait_recv()

    def sent(send, zp):
        for part in range(PARTS):
            transfer(send, A_NEAR, A_NEAR, zp, sibling, part).wait_send()

    def unit(which):
        values = raw[which].astype(jnp.float32)
        inverse = lax.rsqrt(jnp.sum(values * values, axis=-1, keepdims=True) + 1e-06)
        return values * inverse, inverse

    barrier = pltpu.get_barrier_semaphore()
    for device in (sibling, after_same, before_same, before_other):
        pl.semaphore_signal(barrier, inc=1, device_id=device, device_id_type=MESH)

    @pl.when(z < deep - 1)
    def _():
        pl.semaphore_signal(barrier, inc=1, device_id=above, device_id_type=MESH)

    @pl.when(z > 0)
    def _():
        pl.semaphore_signal(barrier, inc=1, device_id=below, device_id_type=MESH)

    for copy in copies:
        copy.wait()
    held[slot(B_NEAR, z)] = unit(core)[0].astype(jnp.bfloat16)
    edges = jnp.where(z > 0, 1, 0) + jnp.where(z < deep - 1, 1, 0)
    pl.semaphore_wait(barrier, 4 + edges)

    def pass_b(zp, distance, part):
        @pl.when(has_b(zp) & (distance > 0))
        def _():
            arrived(B_NEAR, zp, part)

        @pl.when(b_goes_up(zp))
        def _():
            transfer(B_UP, B_NEAR, B_NEAR, zp, above, part).start()

        @pl.when(b_goes_down(zp))
        def _():
            transfer(B_DOWN, B_NEAR, B_NEAR, zp, below, part).start()

        @pl.when(b_to_column(zp))
        def _():
            transfer(B_COLUMN, B_NEAR, B_FAR, zp, before_other, part).start()

    def pass_a(zp, distance, part):
        @pl.when(has_a(zp) & (distance > 0))
        def _():
            arrived(A_NEAR, zp, part)

        @pl.when(a_goes_up(zp))
        def _():
            transfer(A_UP, A_NEAR, A_NEAR, zp, above, part).start()

        @pl.when(a_goes_down(zp))
        def _():
            transfer(A_DOWN, A_NEAR, A_NEAR, zp, below, part).start()

        @pl.when(a_to_column(zp))
        def _():
            transfer(A_COLUMN, A_NEAR, A_FAR, zp, after_same, part).start()

        @pl.when(has_a(zp))
        def _():
            transfer(A_CORE, A_NEAR, X_NEAR, zp, sibling, part).start()

    def relay():
        for part in range(PARTS):
            arrived(B_FAR, z, part)
            transfer(B_RELAY, B_FAR, B_FAR, z, inner, part).start()

            @pl.when(a_end)
            def _():
                arrived(A_FAR, z, part)
                transfer(A_RELAY, A_FAR, A_FAR, z, inner, part).start()

    def sum_copy():
        return pltpu.make_async_remote_copy(
            src_ref=sums.at[0],
            dst_ref=sums.at[1],
            send_sem=sum_sem.at[0],
            recv_sem=sum_sem.at[1],
            device_id=outer,
            device_id_type=MESH,
        )

    def loss_copy():
        return pltpu.make_async_remote_copy(
            src_ref=loss_row.at[0],
            dst_ref=loss_row.at[1],
            send_sem=sum_sem.at[2],
            recv_sem=sum_sem.at[3],
            device_id=outer,
            device_id_type=MESH,
        )

    diagonal = lax.broadcasted_iota(jnp.int32, (rows, rows), 0) == lax.broadcasted_iota(
        jnp.int32, (rows, rows), 1
    )

    def weigh(role, own, other, pairs, with_loss):
        dots = lax.dot_general(
            held[own],
            held[other],
            (((1,), (1,)), ((), ())),
            preferred_element_type=jnp.float32,
        )
        if not with_loss:
            power = jnp.exp2(dots * (-LOG2E * scale) - LOG2E * offset)
            return (scale / (1.0 + power)).astype(jnp.bfloat16)
        logits = scale * dots + offset
        turned = jnp.where(diagonal, -logits, logits) if pairs else logits
        small = jnp.exp(-jnp.abs(turned))
        loss = jnp.maximum(turned, 0.0) + jnp.log1p(small)
        part = loss[:, :LANES]
        for at in range(LANES, rows, LANES):
            part = part + loss[:, at : at + LANES]
        losses[role] += part
        weights = jnp.where(turned >= 0.0, scale, scale * small) / (1.0 + small)
        if pairs:
            weights = jnp.where(diagonal, -weights, weights)
        return weights.astype(jnp.bfloat16)

    def meet(role, own, other, pairs):
        def add(with_loss):
            weights = weigh(role, own, other, pairs, with_loss)
            step = 384 if width % 384 == 0 else width
            for at in range(0, width, step):
                total[role, :, at : at + step] += jnp.dot(
                    weights, held[other, :, at : at + step], preferred_element_type=jnp.float32
                )

        if pairs:
            add(True)
            return
        of_image = (role == core) | ((role == 2) & (z == 1))

        @pl.when(of_image)
        def _():
            add(True)

        @pl.when(jnp.logical_not(of_image))
        def _():
            add(False)

    own_a, own_b = slot(A_NEAR, z), slot(B_NEAR, z)

    def in_row(role):
        return lax.dot_general(
            jnp.ones((8, LANES), jnp.float32),
            losses[role],
            (((1,), (1,)), ((), ())),
            precision=lax.Precision.HIGHEST,
            preferred_element_type=jnp.float32,
        )

    def near(zp):
        first = jnp.where(short(zp), 0, jnp.where(beyond(zp), 1, 0))

        def tile(which, carry):
            @pl.when((which == 2) & has_x(zp))
            def _():
                for part in range(PARTS):
                    arrived(X_NEAR, zp, part)

            role = jnp.where(which == 0, 0, 1)
            kind = jnp.where(which == 0, A_NEAR, jnp.where(which == 1, B_NEAR, X_NEAR))
            own = jnp.where(which == 0, own_b, own_a)

            @pl.when((which < 2) & (zp == z))
            def _():
                meet(role, own, slot(kind, zp), True)

            @pl.when(((which == 2) & has_x(zp)) | ((which == first) & (zp != z)))
            def _():
                meet(role, own, slot(kind, zp), False)

            return carry

        lax.fori_loop(0, 3, tile, 0)

    def far(zp):
        @pl.when(has_b_far(zp))
        def _():
            for part in range(PARTS):

                @pl.when(jnp.logical_not(at_end & (zp == z)))
                def _():
                    arrived(B_FAR, zp, part)

                @pl.when(crosses(zp))
                def _():
                    transfer(F_CORE, B_FAR, F_FAR, zp, sibling, part).start()

        helps = helper & (zp != end) & (zp != last)

        def tile(which, carry):
            for part in range(PARTS):

                @pl.when((which == 1) & crosses(zp))
                def _():
                    arrived(A_FAR, zp, part)

                @pl.when((which == 1) & has_f(zp))
                def _():
                    arrived(F_FAR, zp, part)

            helping = which < 2
            kind_0 = jnp.where(q_helper, X_NEAR, B_FAR)
            kind_1 = jnp.where(q_helper, F_FAR, A_FAR)
            kind_3 = jnp.where(short(zp), F_FAR, A_FAR)
            kind = jnp.where(
                which == 0,
                kind_0,
                jnp.where(which == 1, kind_1, jnp.where(which == 2, B_FAR, kind_3)),
            )
            in_q = (which == 3) & short(zp)
            own_end = jnp.where(q_helper, slot(A_NEAR, end), slot(B_NEAR, end))
            own = jnp.where(helping, own_end, jnp.where(in_q, own_a, own_b))
            role = jnp.where(helping, 2, jnp.where(in_q, 1, 0))
            other = (zp != z) & (through(zp) | jnp.logical_not(at_end))

            @pl.when(
                (helping & helps)
                | ((which == 2) & has_b_far(zp))
                | ((which == 3) & other)
            )
            def _():
                meet(role, own, slot(kind, zp), False)

            @pl.when((which == 1) & helper & (zp == final))
            def _():
                sums[0] = total[2].astype(jnp.bfloat16)
                sum_copy().start()

                @pl.when(z == 1)
                def _():
                    loss_row[0] = in_row(2)
                    loss_copy().start()

            return carry

        lax.fori_loop(0, 4, tile, 0)

    inward = jnp.where(z < deep // 2, 1, -1)

    def both_ways(distance, action):
        ahead, behind = z + inward * distance, z - inward * distance

        @pl.when((distance >= 0) & (distance < deep) & (ahead >= 0) & (ahead < deep))
        def _():
            action(ahead)

        @pl.when((distance > 0) & (behind >= 0) & (behind < deep))
        def _():
            action(behind)

    def turn(distance, carry):
        for part in range(PARTS):
            both_ways(distance, functools.partial(pass_b, distance=distance, part=part))

        @pl.when(distance == 0)
        def _():
            held[slot(A_NEAR, z)] = unit(1 - core)[0].astype(jnp.bfloat16)

        for part in range(PARTS):
            both_ways(distance, functools.partial(pass_a, distance=distance, part=part))

        @pl.when(distance == 0)
        def _():
            total[...] = jnp.zeros_like(total)
            losses[...] = jnp.zeros_like(losses)

        both_ways(distance, near)
        pl.when((distance == 0) & at_end)(relay)
        both_ways(distance - 1, far)
        return carry

    lax.fori_loop(0, deep + 1, turn, 0)

    def finish(which, role, ref):
        unit32, inverse = unit(which)
        grad = total[role]
        along = jnp.sum(unit32 * grad, axis=-1, keepdims=True)
        ref[...] = inverse * (grad - unit32 * along)

    def finish_images():
        finish(0, core, grad_img_ref)

    def finish_texts():
        finish(1, 1 - core, grad_txt_ref)

    pl.when(z == 0)(finish_texts)
    pl.when(z != 0)(finish_images)

    @pl.when(at_end)
    def _():
        sum_copy().wait_recv()
        role = jnp.where(a_end, 1, 0)
        total[role] += sums[1].astype(jnp.float32)

    pl.when(z == 0)(finish_images)
    pl.when(z != 0)(finish_texts)
    loss_ref[...] = in_row(core)[0:1]

    @pl.when(z == 0)
    def _():
        loss_copy().wait_recv()
        loss_ref[...] += loss_row[1, 0:1]

    def settle(zp, carry):
        for went, send in (
            (a_goes_up(zp), A_UP),
            (a_goes_down(zp), A_DOWN),
            (b_goes_up(zp), B_UP),
            (b_goes_down(zp), B_DOWN),
            (has_a(zp), A_CORE),
            (a_to_column(zp), A_COLUMN),
            (b_to_column(zp), B_COLUMN),
            (crosses(zp), F_CORE),
            ((zp == z) & a_end, A_RELAY),
            ((zp == z) & at_end, B_RELAY),
        ):
            pl.when(went)(functools.partial(sent, send, zp))
        return carry

    lax.fori_loop(0, deep, settle, 0)

    @pl.when(helper)
    def _():
        sum_copy().wait_send()
        pl.when(z == 1)(lambda: loss_copy().wait_send())


def on_column(columns, deep, images, texts, scale, offset):
    rows, width = images.shape
    tiles = 4 * deep
    loss, grad_images, grad_texts = pl.pallas_call(
        functools.partial(column_kernel, columns, deep),
        out_shape=(
            jax.ShapeDtypeStruct((1, rows), jnp.float32),
            jax.ShapeDtypeStruct((rows, width), jnp.float32),
            jax.ShapeDtypeStruct((rows, width), jnp.float32),
        ),
        in_specs=[pl.BlockSpec(memory_space=pltpu.SMEM)] * 2
        + [pl.BlockSpec(memory_space=pl.ANY)] * 2,
        out_specs=[pl.BlockSpec(memory_space=pltpu.VMEM)] * 3,
        scratch_shapes=[
            pltpu.VMEM((KINDS * deep, rows, width), jnp.bfloat16),
            pltpu.VMEM((3, rows, width), jnp.float32),
            pltpu.VMEM((3, rows, LANES), jnp.float32),
            pltpu.VMEM((2, rows, width), jnp.bfloat16),
            pltpu.VMEM((2, 8, rows), jnp.float32),
            pltpu.VMEM((2, rows, width), jnp.bfloat16),
            pltpu.SemaphoreType.DMA((2,)),
            pltpu.SemaphoreType.DMA((SENDS * deep, PARTS)),
            pltpu.SemaphoreType.DMA((KINDS * deep, PARTS)),
            pltpu.SemaphoreType.DMA((4,)),
        ],
        compiler_params=pltpu.CompilerParams(
            collective_id=0, has_side_effects=True, vmem_limit_bytes=60 * 1024 * 1024
        ),
        cost_estimate=pl.CostEstimate(
            flops=tiles * 4 * rows * rows * width,
            bytes_accessed=12 * rows * width,
            transcendentals=tiles * 3 * rows * rows,
        ),
        name="column",
    )(scale, offset, images, texts)
    return loss.reshape(rows), grad_images, grad_texts


def solution(mesh):
    blocks, deep = mesh.shape["blk"], mesh.shape["grp"]
    body = on_device
    if KSTEPS == 2 * deep and deep >= 4 and blocks % 2 == 0 and blocks >= 6:
        body = functools.partial(on_column, blocks // 2, deep)
    return jax.shard_map(
        body,
        mesh=mesh,
        in_specs=(P(("blk", "grp"), None), P(("blk", "grp"), None), P(), P()),
        out_specs=(P(("blk", "grp")), P(("blk", "grp"), None), P(("blk", "grp"), None)),
        check_vma=False,
    )
```
